512 devices in a mesh: coil: 8 (over y), slab: 64 (over x, z, core).
Axes of the slice: x: 4, y: 8, z: 8, core: 2. Of those that a mesh axis runs over, the one named last changes fastest.
Arguments:
- kspace: float32 [2, 32, 384, 8, 384], P(None, 'coil', 'slab'), may hold values from -6 to 6
- coil_maps: bfloat16 [2, 32, 384, 8, 384], P(None, 'coil', 'slab'), may hold values from -0.75 to 0.75, as said below
- sampling: int32 [384, 384], P('slab'), may hold values 0 or 1
- variation_weights: float32 [3, 384, 8, 384], P(None, 'slab', 'coil'), may hold values from 0.02 to 0.2
Outputs:
- solution_image: float32 [2, 384, 8, 384], P(None, 'slab', 'coil')
- residual: float32 [2, 384, 8, 384], P(None, 'slab', 'coil')
The draws below stay inside these ranges and needn't reach their ends.
Inputs may be any that keep to these rules, and one draw needn't show every extreme that they name: `coil_maps`: the sensitivities are bounded in magnitude. `sampling`: each phase encoding is acquired or not.
All inputs are finite; a program needn't handle non-finite values. No bound on the sum of `sampling` on one device may be relied on, other than what follows from the above.
Results may differ from the reference program's by a relative error of at most 0.008.
Values sent between devices are 32-bit elements; how exact they have to be, the bound alone decides.
A program may use at most 128 MiB of HBM per device.

```python
import math
import jax
import jax.numpy as jnp
from jax import lax

NY = 384
NZ = 384
XS = 8
ITERS = 2
COILS = 32


def draw_coil_maps(key, part):
    key = jax.random.fold_in(key, 7)
    depth_frac = jnp.arange(NZ, dtype=jnp.float32) / NZ
    profile = jnp.exp(depth_frac * 1.0986)[None, None, :, None, None]
    values = jax.random.uniform(key, (2, COILS, NZ, XS, NY), jnp.float32, -1.0, 1.0)
    return (0.25 * profile * values).astype(jnp.bfloat16)


def with_ends(drawn, stream_key, low, top_value):
    longest = drawn.shape.index(max(drawn.shape))
    spots = []
    for shift in (0, 1):
        where = [jax.random.randint(jax.random.fold_in(stream_key, axis), (), 0, length) for axis, length in enumerate(drawn.shape)]
        where[longest] = (where[longest] + shift) % drawn.shape[longest]
        spots.append(tuple(where))
    return drawn.at[spots[0]].set(low).at[spots[1]].set(top_value)


def levels(own_key, extent, cuts, low, high):
    def one(position, parts):
        draws = jax.random.uniform(jax.random.fold_in(jax.random.fold_in(own_key, 6), position), (parts,), jnp.float32, low / len(cuts), high / len(cuts))
        return jnp.repeat(jnp.exp(draws), extent[position] // parts).reshape((-1,) + (1,) * (len(extent) - position - 1))

    loudness = one(*cuts[0])
    for cut in cuts[1:]:
        loudness = loudness * one(*cut)
    return loudness


def gaussian(own_key, shape, scale, limit, cuts=(), held_as=jnp.bfloat16):
    drawn = scale * jax.random.normal(own_key, shape, jnp.float32)
    if cuts:
        drawn = drawn * levels(own_key, shape, cuts, -0.22, 0.18)
    return jnp.clip(drawn, -limit, limit).astype(held_as)


def setup_inputs(seed: int = 0) -> dict:
    key_list = jax.random.split(jax.random.key(seed), 5)
    return {
        "kspace": gaussian(key_list[0], (2, COILS, NY, XS, NZ), 1.0, 6.0, ((1, 8), (2, 64)), jnp.float32),
        "coil_maps": draw_coil_maps(jax.random.fold_in(key_list[4], 71), 0),
        "sampling": with_ends((jax.random.randint(key_list[2], (NY, NZ), 0, 3) < 1).astype(jnp.int32), jax.random.fold_in(key_list[2], 1), 0, 1),
        "variation_weights": jnp.clip(jnp.exp(math.log(0.2) - 2.3025851 * jax.random.uniform(key_list[3], (3, NZ, XS, NY), jnp.float32) ** levels(key_list[3], (3, NZ, XS, NY), ((1, 64), (2, 8)), -0.2, 0.2)), 0.02, 0.2),
    }


def variation_term(padded, halo_weights):
    summed = 0.0
    for axis_dim in (1, 2, 3):
        inner_part = padded
        inner_weight = halo_weights[axis_dim - 1]
        for other_dim in (1, 2, 3):
            if other_dim != axis_dim:
                inner_part = lax.slice_in_dim(inner_part, 1, inner_part.shape[other_dim] - 1, axis=other_dim)
                inner_weight = lax.slice_in_dim(inner_weight, 1, inner_weight.shape[other_dim - 1] - 1, axis=other_dim - 1)
        length = inner_part.shape[axis_dim] - 2
        jumps = lax.slice_in_dim(inner_part, 1, length + 2, axis=axis_dim) - lax.slice_in_dim(inner_part, 0, length + 1, axis=axis_dim)
        fluxes = lax.slice_in_dim(inner_weight, 0, length + 1, axis=axis_dim - 1)[None] * jumps
        summed = summed + lax.slice_in_dim(fluxes, 0, length, axis=axis_dim) - lax.slice_in_dim(fluxes, 1, length + 1, axis=axis_dim)
    return summed


def to_pair(values):
    return jnp.stack([jnp.real(values), jnp.imag(values)])


def sensitivity(coil_map):
    return lax.complex(coil_map[0].astype(jnp.float32), coil_map[1].astype(jnp.float32))


def reference(kspace, coil_maps, sampling, variation_weights):
    sampled = jnp.transpose(sampling).astype(jnp.float32)[:, None, :]
    maps_first = jnp.moveaxis(coil_maps, 1, 0)
    data_first = jnp.moveaxis(kspace, 1, 0)
    zeros_field = jnp.zeros((NZ, XS, NY), jnp.float32)
    empty = lax.complex(zeros_field, zeros_field)
    padding = ((0, 0), (1, 1), (1, 1), (1, 1))
    halo_weights = jnp.pad(variation_weights, padding)

    def adjoint_step(summed, pieces):
        coil_map, measured = pieces
        spectrum = jnp.transpose(lax.complex(measured[0], measured[1]), (2, 1, 0))
        back = jnp.fft.ifftn(spectrum * sampled, axes=(0, 2), norm="ortho")
        return summed + jnp.conj(sensitivity(coil_map)) * back, None

    def operator(field_pair):
        image_now = lax.complex(field_pair[0], field_pair[1])

        def normal_step(summed, coil_map):
            coil_sens = sensitivity(coil_map)
            spectrum = jnp.fft.fftn(coil_sens * image_now, axes=(0, 2), norm="ortho")
            back = jnp.fft.ifftn(spectrum * sampled, axes=(0, 2), norm="ortho")
            return summed + jnp.conj(coil_sens) * back, None

        summed, _ = lax.scan(normal_step, empty, maps_first)
        return to_pair(summed) + variation_term(jnp.pad(field_pair, padding), halo_weights)

    adjoint, _ = lax.scan(adjoint_step, empty, (maps_first, data_first))
    residual = to_pair(adjoint)
    direction = residual
    solution_image = jnp.zeros_like(residual)
    norm_now = jnp.sum(residual * residual)
    for iteration in range(ITERS):
        operated = operator(direction)
        step_size = norm_now / jnp.sum(direction * operated)
        solution_image = solution_image + step_size * direction
        residual = residual - step_size * operated
        norm_next = jnp.sum(residual * residual)
        direction = residual + (norm_next / norm_now) * direction
        norm_now = norm_next
    return solution_image, residual
```

```python
from functools import partial
import math

import jax
import jax.numpy as jnp
import numpy as np
from jax import lax
from jax.experimental import pallas as pl
from jax.experimental.pallas import tpu as pltpu
from jax.sharding import PartitionSpec as P

F32 = jnp.float32
BF16 = jnp.bfloat16
PAD = 8


def halves(table):
    high = table.astype(BF16)
    low = (table - high.astype(np.float32)).astype(BF16)
    return np.stack([high, low])


def fourier_tables(length, chips, planes):
    natural = np.arange(length, dtype=np.int64)
    core, chip, plane = np.meshgrid(np.arange(2), np.arange(chips), np.arange(PAD), indexing="ij")
    owned = (chip * 2 + core) * planes + plane
    valid = (plane < planes).astype(np.float64).reshape(2, 1, -1)
    angles = natural[None, :, None] * owned.reshape(2, 1, -1) % length * (2.0 * math.pi / length)
    cosine = np.cos(angles) * valid / math.sqrt(length)
    sine = np.sin(angles) * valid / math.sqrt(length)
    right = np.concatenate(
        [np.concatenate([cosine, -sine], axis=2), np.concatenate([sine, cosine], axis=2)], axis=1
    )
    left = np.concatenate(
        [np.concatenate([cosine, sine], axis=2), np.concatenate([-sine, cosine], axis=2)], axis=1
    )
    back = np.swapaxes(left, 1, 2)
    home = np.swapaxes(right, 1, 2)
    return tuple(halves(table.astype(np.float32)) for table in (right, left, back, home))


def split(value):
    high = value.astype(BF16)
    return high, (value - high.astype(F32)).astype(BF16)


def dot(a, b):
    return jnp.dot(a, b, preferred_element_type=F32)


def times_table(value, table, which):
    high, low = value
    return (
        dot(high, table[0, which]) + dot(low, table[0, which]) + dot(high, table[1, which])
    )


def table_times(table, which, value):
    high, low = value
    return (
        dot(table[0, which], high) + dot(table[0, which], low) + dot(table[1, which], high)
    )


def kernel(
    sizes,
    k_ref, s_ref, m_ref, w_ref, right_hbm, left_hbm, back_hbm, home_hbm,
    x_out, r_out,
    right, left, back, home,
    ky, kz, kx, sy, sz, sx, mb,
    mask_t, s_pad, v_pad, k_pad,
    t_send, t_recv, u_send, u_recv,
    part, rx, q, rz, ag,
    wz_send, wz_recv, wx_recv, hz_send, hz_recv, hx_recv,
    frame, xframe, wframe,
    ar_y, ar_z, ar_x,
    table_sem,
    y_send, y_recv, z_send, z_recv, x_send, x_recv,
    mz_send, mz_recv, mx_send, mx_recv,
    agz_send, agz_recv, agx_send, agx_recv,
    rsx_send, rsx_recv, rsz_send, rsz_recv,
    core_send, core_recv,
    w_send, w_recv, halo_send, halo_recv,
    ary_send, ary_recv, arz_send, arz_recv, arx_send, arx_recv,
):
    gx, gy, gz, planes, length = sizes
    chips = gx * gz
    rows = chips * PAD
    y = lax.axis_index("coil")
    slab = lax.axis_index("slab")
    x = slab // (gz * 2)
    z = (slab // 2) % gz
    h = slab % 2
    other = 1 - h

    def device(y_, x_, z_, h_):
        return (y_, (x_ * gz + z_) * 2 + h_)

    def remote(src, dst, send_sem, recv_sem, target):
        return pltpu.make_async_remote_copy(
            src_ref=src, dst_ref=dst, send_sem=send_sem, recv_sem=recv_sem,
            device_id=target, device_id_type=pl.DeviceIdType.MESH,
        )

    sibling = device(y, x, z, other)

    def got(dst, recv_sem):
        remote(dst, dst, recv_sem, recv_sem, sibling).wait_recv()

    def sent(src, send_sem):
        remote(src, src, send_sem, send_sem, sibling).wait_send()

    def along_y(d):
        return (y + d) % gy

    def along_z(d):
        return (z + d) % gz

    def along_x(d):
        return (x + d) % gx

    table_copies = [
        pltpu.make_async_copy(src, dst, table_sem.at[i])
        for i, (src, dst) in enumerate(
            ((back_hbm, back), (home_hbm, home), (right_hbm, right), (left_hbm, left))
        )
    ]
    for copy in table_copies:
        copy.start()

    slabs = gx * gz * 2
    below = (slab + slabs - 1) % slabs
    above = (slab + 1) % slabs
    barrier = pltpu.get_barrier_semaphore()

    def greet(target):
        pl.semaphore_signal(barrier, inc=1, device_id=target, device_id_type=pl.DeviceIdType.MESH)

    for d in range(1, gy):
        greet(device(along_y(d), x, z, h))
    for d in range(1, gz):
        greet(device(y, x, along_z(d), h))
    for d in range(1, gx):
        greet(device(y, along_x(d), z, h))
        greet(device(y, along_x(d), z, other))
    greet(sibling)
    greet((y, jnp.where(h == 0, below, above)))
    pl.semaphore_wait(barrier, (gy - 1) + (gz - 1) + 2 * (gx - 1) + 2)

    arrays = ((k_ref, ky, kz, kx), (s_ref, sy, sz, sx))

    for i, (src, slots, _, _) in enumerate(arrays):
        for d in range(1, gy):
            to = along_y(d)
            remote(
                src.at[to], slots.at[y], y_send.at[i], y_recv.at[i, y], device(to, x, z, h)
            ).start()

    mb[x, z] = m_ref[...]
    for d in range(1, gz):
        remote(
            mb.at[x, z], mb.at[x, z], mz_send, mz_recv.at[z], device(y, x, along_z(d), h)
        ).start()
    wz_send[0:1, :] = w_ref[0, planes - 1 : planes, :]
    remote(wz_send, wz_recv, w_send.at[0], w_recv.at[0], (y, above)).start()
    remote(w_ref.at[1], wx_recv, w_send.at[1], w_recv.at[1], device(along_y(1), x, z, h)).start()

    for i, (src, slots, _, _) in enumerate(arrays):
        slots[y] = src[y]
    k_pad[...] = jnp.zeros_like(k_pad)
    s_pad[...] = jnp.zeros_like(s_pad)
    v_pad[...] = jnp.zeros_like(v_pad)

    def forward_z(i):
        _, slots, next_slots, _ = arrays[i]

        def arrived(source):
            @pl.when(source != y)
            def _():
                got(slots.at[source], y_recv.at[i, source])

        @pl.loop(1, gz)
        def _(d):
            to = along_z(d)
            arrived(to)
            remote(
                slots.at[to], next_slots.at[z], z_send.at[i], z_recv.at[i, z],
                device(y, x, to, h),
            ).start()

        arrived(z)
        next_slots[z] = slots[z]

    def forward_x(i):
        _, _, slots, last_slots = arrays[i]

        @pl.loop(0, gz)
        def _(d):
            source = along_z(d)

            @pl.when(d != 0)
            def _():
                got(slots.at[source], z_recv.at[i, source])

            for f in range(1, gx):
                to = along_x(f)
                remote(
                    slots.at[source, to], last_slots.at[x, source], x_send.at[i], x_recv.at[i],
                    device(y, to, z, h),
                ).start()
            last_slots[x, source] = slots[source, x]

    def gather_x(slots, z_recv_sem, x_send_sem, x_recv_sem):
        @pl.loop(0, gz)
        def _(d):
            source = along_z(d)

            @pl.when(d != 0)
            def _():
                got(slots.at[x, source], z_recv_sem.at[source])

            for f in range(1, gx):
                remote(
                    slots.at[x, source], slots.at[x, source], x_send_sem, x_recv_sem,
                    device(y, along_x(f), z, h),
                ).start()

        got(slots.at[pl.ds(0, gx - 1)], x_recv_sem)

    forward_z(0)
    gather_x(mb, mz_recv, mx_send, mx_recv)
    forward_x(0)
    forward_z(1)

    def padded(ref, index):
        return ref[index].reshape(rows, length)

    k_pad[0, :, 0:planes, :] = mb[...].reshape(chips, planes, length)
    mask_t[...] = padded(k_pad, 0).T
    got(kx.at[pl.ds(0, gx - 1)], x_recv.at[0])
    for c in range(2):
        k_pad[c, :, 0:planes, :] = kx[:, :, c].reshape(chips, planes, length)
    spectrum = jnp.concatenate([padded(k_pad, 0).T, padded(k_pad, 1).T], axis=0)

    def to_image(spectrum, use, between):
        pieces = split(spectrum)
        if use == 0:
            table_copies[0].wait()
        u_send[use] = table_times(back, other, pieces)
        swap = remote(
            u_send.at[use], u_recv.at[use], core_send.at[use], core_recv.at[use], sibling
        )
        swap.start()
        mine = table_times(back, h, pieces)
        if use == 0:
            table_copies[1].wait()
        between()

        def home_of(value, which):
            wide = jnp.concatenate([value[0:rows], value[rows : 2 * rows]], axis=1)
            return times_table(split(wide), home, which)

        image = home_of(mine, h)
        swap.wait_recv()
        return image + home_of(u_recv[use], other)

    def coil_sum(image, use):
        re, im = image[:, 0:length], image[:, length : 2 * length]
        s_re, s_im = padded(s_pad, 0), padded(s_pad, 1)
        sums = (s_re * re + s_im * im, s_re * im - s_im * re)
        for c in range(2):
            block = sums[c].reshape(gx, gz, PAD, length)[:, :, 0:planes, :]
            part[use, :, :, c] = block
        for f in range(1, gx):
            to = along_x(f)
            remote(
                part.at[use, to], rx.at[use, x], rsx_send.at[use], rsx_recv.at[use, x],
                device(y, to, z, h),
            ).start()
        total = part[use, x]
        for f in range(1, gx):
            source = along_x(f)
            got(rx.at[use, source], rsx_recv.at[use, source])
            total = total + rx[use, source]
        q[use] = total
        for d in range(1, gz):
            to = along_z(d)
            remote(
                q.at[use, to], rz.at[use, z], rsz_send.at[use], rsz_recv.at[use, z],
                device(y, x, to, h),
            ).start()
        block = q[use, z]
        for d in range(1, gz):
            source = along_z(d)
            got(rz.at[use, source], rsz_recv.at[use, source])
            block = block + rz[use, source]
        return block

    def start_gather(block, it):
        ag[it, x, z] = block
        own = ag.at[it, x, z]
        for d in range(1, gz):
            remote(
                own, own, agz_send.at[it], agz_recv.at[it, z], device(y, x, along_z(d), h)
            ).start()
        hz_send[it, 0, :, :] = block[:, 0, :]
        hz_send[it, 1, :, :] = block[:, planes - 1, :]
        for i, target in enumerate(((y, below), (y, above))):
            remote(
                hz_send.at[it, i], hz_recv.at[it, i], halo_send.at[it, i], halo_recv.at[it, i],
                target,
            ).start()
        for i, d in enumerate((gy - 1, 1)):
            remote(
                own, hx_recv.at[it, i], halo_send.at[it, 2 + i], halo_recv.at[it, 2 + i],
                device(along_y(d), x, z, h),
            ).start()

    row_ids = lax.broadcasted_iota(jnp.int32, (PAD, length), 0)
    lane_ids = lax.broadcasted_iota(jnp.int32, (PAD, length), 1)

    def variation(block, it):
        for i in range(2):
            got(hz_recv.at[it, i], halo_recv.at[it, i])
            got(hx_recv.at[it, i], halo_recv.at[it, 2 + i])
        first = (slab > 0).astype(F32)
        last = (slab < slabs - 1).astype(F32)
        x_first = (y > 0).astype(F32)
        x_last = (y < gy - 1).astype(F32)
        frame[:, 1 : planes + 1, :] = block
        frame[:, planes + 1, :] = hz_recv[it, 0] * last
        frame[:, 0, :] = hz_recv[it, 1] * first
        xframe[0, :, 1 : planes + 1, :] = hx_recv[it, 0] * x_last
        xframe[1, :, 1 : planes + 1, :] = hx_recv[it, 1] * x_first
        for c in range(2):
            v = frame[c]
            flux = wframe[0] * (pltpu.roll(v, PAD - 1, 0) - v)
            out = pltpu.roll(flux, 1, 0) - flux
            out = out + wframe[2] * (v - xframe[1, c]) - wframe[1] * (xframe[0, c] - v)
            ahead = jnp.where(lane_ids < length - 1, pltpu.roll(v, length - 1, 1), 0.0)
            flux = wframe[3] * (ahead - v)
            out = out + jnp.where(lane_ids > 0, pltpu.roll(flux, 1, 1), 0.0) - flux
            frame[c] = out
        return frame[:, 1 : planes + 1, :]

    def lanes(value):
        flat = value.reshape(-1, length) if value.ndim == 2 else value
        while flat.ndim > 2:
            flat = jnp.sum(flat, axis=0)
        flat = jnp.sum(flat, axis=0, keepdims=True)
        width = ar_y.shape[-1]
        folded = flat[:, 0:width]
        for i in range(1, flat.shape[1] // width):
            folded = folded + flat[:, i * width : (i + 1) * width]
        return folded

    tile_rows = lax.broadcasted_iota(jnp.int32, ar_y.shape[2:], 0)

    def start_sums(values, it):
        tile = jnp.zeros(ar_y.shape[2:], F32)
        for i, value in enumerate(values):
            tile = jnp.where(tile_rows == i, value, tile)
        ar_y[it, y] = tile
        for d in range(1, gy):
            remote(
                ar_y.at[it, y], ar_y.at[it, y], ary_send.at[it], ary_recv.at[it, y],
                device(along_y(d), x, z, h),
            ).start()

    def total_of(slots, it, count):
        total = slots[it, 0]
        for i in range(1, count):
            total = total + slots[it, i]
        return total

    def sums_z(it):
        for d in range(1, gy):
            got(ar_y.at[it, along_y(d)], ary_recv.at[it, along_y(d)])
        ar_z[it, z] = total_of(ar_y, it, gy)
        for d in range(1, gz):
            remote(
                ar_z.at[it, z], ar_z.at[it, z], arz_send.at[it], arz_recv.at[it, z],
                device(y, x, along_z(d), h),
            ).start()

    def sums_x(it):
        for d in range(1, gz):
            got(ar_z.at[it, along_z(d)], arz_recv.at[it, along_z(d)])
        mine = x * 2 + h
        ar_x[it, mine] = total_of(ar_z, it, gz)
        for d in range(1, 2 * gx):
            to = (mine + d) % (2 * gx)
            remote(
                ar_x.at[it, mine], ar_x.at[it, mine], arx_send.at[it], arx_recv.at[it, mine],
                device(y, to // 2, z, to % 2),
            ).start()

    def finish_sums(it, count):
        mine = x * 2 + h
        for d in range(1, 2 * gx):
            source = (mine + d) % (2 * gx)
            got(ar_x.at[it, source], arx_recv.at[it, source])
        total = total_of(ar_x, it, 2 * gx)
        return [jnp.sum(jnp.where(tile_rows == i, total, 0.0)) for i in range(count)]

    def operator(block, it, sums):
        gather_x(ag.at[it], agz_recv.at[it], agx_send.at[it], agx_recv.at[it])
        smooth = variation(block, it)
        for c in range(2):
            v_pad[c, :, 0:planes, :] = ag[it, :, :, c].reshape(chips, planes, length)
        v_re, v_im = padded(v_pad, 0), padded(v_pad, 1)
        s_re, s_im = padded(s_pad, 0), padded(s_pad, 1)
        coil = jnp.concatenate([s_re * v_re - s_im * v_im, s_re * v_im + s_im * v_re], axis=1)
        pieces = split(coil)
        if it == 0:
            table_copies[2].wait()
        t_send[it] = times_table(pieces, right, other)
        swap = remote(
            t_send.at[it], t_recv.at[it], core_send.at[3 + it], core_recv.at[3 + it], sibling
        )
        swap.start()
        mine = times_table(pieces, right, h)
        if it == 0:
            table_copies[3].wait()

        def left_of(value, which):
            tall = jnp.concatenate([value[:, 0:rows], value[:, rows : 2 * rows]], axis=0)
            return table_times(left, which, split(tall))

        spectrum = left_of(mine, h)
        swap.wait_recv()
        spectrum = spectrum + left_of(t_recv[it], other)
        spectrum = jnp.concatenate(
            [spectrum[0:length] * mask_t[...], spectrum[length : 2 * length] * mask_t[...]], axis=0
        )
        power = jnp.sum(spectrum * spectrum, axis=0, keepdims=True)
        width = ar_y.shape[-1]
        folded = power[:, 0:width]
        for i in range(1, power.shape[1] // width):
            folded = folded + power[:, i * width : (i + 1) * width]
        start_sums([folded + lanes(block * smooth)] + sums, it)
        image = to_image(spectrum, 1 + it, lambda: sums_z(it))
        sums_x(it)
        return coil_sum(image, 1 + it) + smooth

    wframe[...] = jnp.zeros_like(wframe)
    frame[...] = jnp.zeros_like(frame)
    xframe[...] = jnp.zeros_like(xframe)
    got(wz_recv, w_recv.at[0])
    got(wx_recv, w_recv.at[1])
    wframe[0, 1 : planes + 1, :] = w_ref[0]
    wframe[0, 0:1, :] = wz_recv[0:1, :] * (slab > 0).astype(F32)
    wframe[1, 1 : planes + 1, :] = w_ref[1]
    wframe[2, 1 : planes + 1, :] = wx_recv[...] * (y > 0).astype(F32)
    wframe[3, 1 : planes + 1, :] = w_ref[2]

    image = to_image(spectrum, 0, lambda: None)
    forward_x(1)
    got(sx.at[pl.ds(0, gx - 1)], x_recv.at[1])
    for c in range(2):
        s_pad[c, :, 0:planes, :] = sx[:, :, c].reshape(chips, planes, length)
    first = coil_sum(image, 0)

    start_gather(first, 0)
    applied = operator(first, 0, [lanes(first * first)])
    curvature, norm = finish_sums(0, 2)
    step = norm / curvature
    second = first - step * applied
    start_gather(second, 1)
    r_out[...] = applied
    x_out[...] = second
    fresh = operator(second, 1, [lanes(second * second), lanes(second * applied)])
    applied = r_out[...]
    second = x_out[...]
    first = ag[0, x, z]
    own, norm_next, cross = finish_sums(1, 3)
    ratio = norm_next / norm
    curvature_next = own + 2.0 * ratio * cross + ratio * ratio * curvature
    step_next = norm_next / curvature_next
    x_out[...] = step * first + step_next * (second + ratio * first)
    r_out[...] = second - step_next * (fresh + ratio * applied)

    for i in range(2):
        sent(ky.at[pl.ds(0, gy - 1)], y_send.at[i])
        sent(kz.at[pl.ds(0, gz - 1)], z_send.at[i])
        sent(kx.at[pl.ds(0, gx - 1)], x_send.at[i])
        sent(ag.at[i, 0, pl.ds(0, gz - 1)], agz_send.at[i])
        sent(ag.at[i, pl.ds(0, gx - 1)], agx_send.at[i])
        sent(ar_y.at[i, pl.ds(0, gy - 1)], ary_send.at[i])
        sent(ar_z.at[i, pl.ds(0, gz - 1)], arz_send.at[i])
        sent(ar_x.at[i, pl.ds(0, 2 * gx - 1)], arx_send.at[i])
        sent(t_send.at[i], core_send.at[3 + i])
        for j in range(2):
            sent(hz_send.at[i, j], halo_send.at[i, j])
            sent(hx_recv.at[i, j], halo_send.at[i, 2 + j])
    for use in range(3):
        sent(rx.at[use, pl.ds(0, gx - 1)], rsx_send.at[use])
        sent(rz.at[use, pl.ds(0, gz - 1)], rsz_send.at[use])
        sent(u_send.at[use], core_send.at[use])
    sent(mb.at[0, pl.ds(0, gz - 1)], mz_send)
    sent(mb.at[pl.ds(0, gx - 1)], mx_send)
    sent(wz_send, w_send.at[0])
    sent(wx_recv, w_send.at[1])


def body(sizes, kspace, coil_maps, sampling, variation_weights):
    gx, gy, gz, planes, length = sizes
    chips = gx * gz
    rows = chips * PAD
    lanes = math.gcd(128, length, rows)
    sampled = sampling.astype(F32)
    k_in = jnp.transpose(kspace * sampled[None, None, :, None, :], (3, 1, 0, 2, 4))
    s_in = jnp.transpose(coil_maps.astype(F32), (3, 1, 0, 2, 4))
    tables = fourier_tables(length, chips, planes)
    block = (2, planes, length)
    wires = (gy, gx) + block
    last = (gx, gz) + block
    dma = pltpu.SemaphoreType.DMA
    vmem = pltpu.VMEM
    scratch = [vmem(table.shape, BF16) for table in tables]
    scratch += [vmem(shape, F32) for shape in (wires, wires, last) * 2]
    scratch += [
        vmem((gx, gz, planes, length), F32),
        vmem((length, rows), F32),
        vmem((2, chips, PAD, length), F32),
        vmem((2, chips, PAD, length), F32),
        vmem((2, chips, PAD, length), F32),
        vmem((2, rows, 2 * rows), F32),
        vmem((2, rows, 2 * rows), F32),
        vmem((3, 2 * rows, rows), F32),
        vmem((3, 2 * rows, rows), F32),
        vmem((3,) + last, F32),
        vmem((3,) + last, F32),
        vmem((3, gz) + block, F32),
        vmem((3, gz) + block, F32),
        vmem((2,) + last, F32),
        vmem((PAD, length), F32),
        vmem((PAD, length), F32),
        vmem((planes, length), F32),
        vmem((2, 2, 2, length), F32),
        vmem((2, 2, 2, length), F32),
        vmem((2, 2) + block, F32),
        vmem((2, PAD, length), F32),
        vmem((2, 2, PAD, length), F32),
        vmem((4, PAD, length), F32),
        vmem((2, gy, 8, lanes), F32),
        vmem((2, gz, 8, lanes), F32),
        vmem((2, 2 * gx, 8, lanes), F32),
        dma((4,)),
        dma((2,)), dma((2, gy)), dma((2,)), dma((2, gz)), dma((2,)), dma((2,)),
        dma(()), dma((gz,)), dma(()), dma(()),
        dma((2,)), dma((2, gz)), dma((2,)), dma((2,)),
        dma((3,)), dma((3, gx)), dma((3,)), dma((3, gz)),
        dma((5,)), dma((5,)),
        dma((2,)), dma((2,)), dma((2, 4)), dma((2, 4)),
        dma((2,)), dma((2, gy)), dma((2,)), dma((2, gz)), dma((2,)), dma((2, 2 * gx)),
    ]
    in_vmem = pl.BlockSpec(memory_space=pltpu.VMEM)
    anywhere = pl.BlockSpec(memory_space=pl.ANY)
    image, residual = pl.pallas_call(
        partial(kernel, sizes),
        out_shape=[jax.ShapeDtypeStruct(block, F32)] * 2,
        in_specs=[in_vmem] * 4 + [anywhere] * 4,
        out_specs=[in_vmem] * 2,
        scratch_shapes=scratch,
        compiler_params=pltpu.CompilerParams(
            collective_id=0, has_side_effects=True, vmem_limit_bytes=58 * 2**20
        ),
    )(k_in, s_in, sampled, variation_weights[:, :, 0, :], *[jnp.asarray(t) for t in tables])
    return image[:, :, None, :], residual[:, :, None, :]


def solution(mesh, gx=4, gz=8):
    gy = mesh.shape["coil"]

    def whole(kspace, coil_maps, sampling, variation_weights):
        length = kspace.shape[4]
        sizes = (gx, gy, gz, length // (gx * gz * 2), length)
        return jax.shard_map(
            partial(body, sizes),
            mesh=mesh,
            in_specs=(
                P(None, "coil", "slab", None, None),
                P(None, "coil", "slab", None, None),
                P("slab", None),
                P(None, "slab", "coil", None),
            ),
            out_specs=(P(None, "slab", "coil", None), P(None, "slab", "coil", None)),
            check_vma=False,
        )(kspace, coil_maps, sampling, variation_weights)

    return whole
```

```python
from functools import partial
import math

import jax
import jax.numpy as jnp
import numpy as np
from jax import lax
from jax.experimental import pallas as pl
from jax.experimental.pallas import tpu as pltpu
from jax.sharding import PartitionSpec as P

F32 = jnp.float32
BF16 = jnp.bfloat16
PAD = 8


def halves(table):
    high = table.astype(BF16)
    low = (table - high.astype(np.float32)).astype(BF16)
    return np.stack([high, low])


def fourier_tables(length, chips, planes):
    natural = np.arange(length, dtype=np.int64)
    core, chip, plane = np.meshgrid(np.arange(2), np.arange(chips), np.arange(PAD), indexing="ij")
    owned = (chip * 2 + core) * planes + plane
    valid = (plane < planes).astype(np.float64).reshape(2, 1, -1)
    angles = natural[None, :, None] * owned.reshape(2, 1, -1) % length * (2.0 * math.pi / length)
    cosine = np.cos(angles) * valid / math.sqrt(length)
    sine = np.sin(angles) * valid / math.sqrt(length)
    right = np.concatenate(
        [np.concatenate([cosine, -sine], axis=2), np.concatenate([sine, cosine], axis=2)], axis=1
    )
    left = np.concatenate(
        [np.concatenate([cosine, sine], axis=2), np.concatenate([-sine, cosine], axis=2)], axis=1
    )
    back = np.swapaxes(left, 1, 2)
    home = np.swapaxes(right, 1, 2)
    return tuple(halves(table.astype(np.float32)) for table in (right, left, back, home))


def split(value):
    high = value.astype(BF16)
    return high, (value - high.astype(F32)).astype(BF16)


def dot(a, b):
    return jnp.dot(a, b, preferred_element_type=F32)


def times_table(value, table, which):
    high, low = value
    return (
        dot(high, table[0, which]) + dot(low, table[0, which]) + dot(high, table[1, which])
    )


def table_times(table, which, value):
    high, low = value
    return (
        dot(table[0, which], high) + dot(table[0, which], low) + dot(table[1, which], high)
    )


def nearest(count):
    offsets = [0]
    for d in range(1, count // 2):
        offsets += [d, -d]
    return offsets + [count // 2]


def kernel(
    sizes,
    k_ref, s_ref, m_ref, w_ref, right_hbm, left_hbm, back_hbm, home_hbm,
    x_out, r_out,
    right, left, back, home,
    wy, wz, kx, sx, mb,
    mask_t, s_pad, v_pad, k_pad,
    t_send, t_recv, u_send, u_recv,
    part, rx, q, rz, ag,
    wz_send, wz_recv, wx_recv, hz_send, hz_recv, hx_recv,
    frame, xframe, wframe, smooth, hold,
    ar_y, ar_z, ar_x,
    table_sem,
    y_send, y_recv, z_send, z_recv, x_send, x_recv,
    agz_send, agz_recv, agx_send, agx_recv,
    rsx_send, rsx_recv, rsz_send, rsz_recv,
    core_send, core_recv,
    w_send, w_recv, halo_send, halo_recv,
    ary_send, ary_recv, arz_send, arz_recv, arx_send, arx_recv,
):
    gx, gy, gz, planes, length, width = sizes
    chips = gx * gz
    rows = chips * PAD
    tiles = length // width
    y = lax.axis_index("coil")
    slab = lax.axis_index("slab")
    x = slab // (gz * 2)
    z = (slab // 2) % gz
    h = slab % 2
    other = 1 - h

    def device(y_, x_, z_, h_):
        return (y_, (x_ * gz + z_) * 2 + h_)

    def remote(src, dst, send_sem, recv_sem, target):
        return pltpu.make_async_remote_copy(
            src_ref=src, dst_ref=dst, send_sem=send_sem, recv_sem=recv_sem,
            device_id=target, device_id_type=pl.DeviceIdType.MESH,
        )

    sibling = device(y, x, z, other)

    def got(dst, recv_sem):
        remote(dst, dst, recv_sem, recv_sem, sibling).wait_recv()

    def sent(src, send_sem):
        remote(src, src, send_sem, send_sem, sibling).wait_send()

    def along_y(d):
        return (y + d + gy) % gy

    def along_z(d):
        return (z + d + gz) % gz

    def along_x(d):
        return (x + d + gx) % gx

    table_copies = [
        pltpu.make_async_copy(src, dst, table_sem.at[i])
        for i, (src, dst) in enumerate(
            ((back_hbm, back), (home_hbm, home), (right_hbm, right), (left_hbm, left))
        )
    ]
    for copy in table_copies:
        copy.start()

    slabs = gx * gz * 2
    below = (slab + slabs - 1) % slabs
    above = (slab + 1) % slabs
    barrier = pltpu.get_barrier_semaphore()

    def greet(target):
        pl.semaphore_signal(barrier, inc=1, device_id=target, device_id_type=pl.DeviceIdType.MESH)

    for d in range(1, gy):
        greet(device(along_y(d), x, z, h))
    for d in range(1, gz):
        greet(device(y, x, along_z(d), h))
    for d in range(1, gx):
        greet(device(y, along_x(d), z, h))
        greet(device(y, along_x(d), z, other))
    greet(sibling)
    greet((y, jnp.where(h == 0, below, above)))
    pl.semaphore_wait(barrier, (gy - 1) + (gz - 1) + 2 * (gx - 1) + 2)

    steps = 2 * gx
    sources = (k_ref, s_ref)
    ends = (kx, sx)

    def over_y(t):
        source, coil = sources[t // gx], along_x(t % gx)
        for d in nearest(gy)[:0:-1]:
            to = along_y(d)
            remote(
                source.at[to, coil], wy.at[t, y], y_send.at[t], y_recv.at[t], device(to, x, z, h)
            ).start()
        wy[t, y] = source[y, coil]

    def over_z(t):
        got(wy.at[t, pl.ds(0, gy - 1)], y_recv.at[t])
        for d in nearest(gz)[:0:-1]:
            to = along_z(d)
            remote(
                wy.at[t, to], wz.at[t, z], z_send.at[t], z_recv.at[t], device(y, x, to, h)
            ).start()
        wz[t, z] = wy[t, z]

    def over_x(t):
        got(wz.at[t, pl.ds(0, gz - 1)], z_recv.at[t])
        end = ends[t // gx]
        if t % gx == 0:
            end[x] = wz[t]
        else:
            remote(
                wz.at[t], end.at[x], x_send.at[t], x_recv.at[t],
                device(y, along_x(t % gx), z, h),
            ).start()

    def arrived(i):
        for f in range(1, gx):
            got(ends[i].at[along_x(gx - f)], x_recv.at[i * gx + f])

    over_y(0)
    over_y(1)

    mb[x, z] = m_ref[...]
    for d in nearest(gz)[1:]:
        remote(
            mb.at[x, z], mb.at[x, z], agz_send.at[2], agz_recv.at[2, z],
            device(y, x, along_z(d), h),
        ).start()
    wz_send[0:1, :] = w_ref[0, planes - 1 : planes, :]
    remote(wz_send, wz_recv, w_send.at[0], w_recv.at[0], (y, above)).start()
    remote(w_ref.at[1], wx_recv, w_send.at[1], w_recv.at[1], device(along_y(1), x, z, h)).start()

    k_pad[...] = jnp.zeros_like(k_pad)
    s_pad[...] = jnp.zeros_like(s_pad)
    v_pad[...] = jnp.zeros_like(v_pad)

    def gather(slots, use):
        for d in nearest(gz):
            block = slots.at[x, along_z(d)]
            if d != 0:
                got(block, agz_recv.at[use, along_z(d)])
            for f in nearest(gx)[:0:-1]:
                remote(
                    block, block, agx_send.at[use], agx_recv.at[use],
                    device(y, along_x(f), z, h),
                ).start()
        got(slots.at[pl.ds(0, gx - 1)], agx_recv.at[use])

    def spans():
        for c in range(2):
            for i in range(tiles):
                first = (c * tiles + i) * planes
                yield c, slice(i * width, (i + 1) * width), slice(first, first + planes)

    def unpack(pad, blocks):
        for c, at, own in spans():
            pad[c, :, 0:planes, at] = blocks[:, :, own, :].reshape(chips, planes, width)

    def padded(ref, index):
        return ref[index].reshape(rows, length)

    def to_lines(spectrum, use):
        pieces = split(spectrum)
        if use == 0:
            table_copies[0].wait()
        u_send[use] = table_times(back, other, pieces)
        remote(
            u_send.at[use], u_recv.at[use], core_send.at[use], core_recv.at[use], sibling
        ).start()
        return table_times(back, h, pieces)

    def to_image(mine, use):
        if use == 0:
            table_copies[1].wait()

        def home_of(value, which):
            wide = jnp.concatenate([value[0:rows], value[rows : 2 * rows]], axis=1)
            return times_table(split(wide), home, which)

        image = home_of(mine, h)
        got(u_recv.at[use], core_recv.at[use])
        return image + home_of(u_recv[use], other)

    def coil_sum(image, use, hooks):
        re, im = image[:, 0:length], image[:, length : 2 * length]
        s_re, s_im = padded(s_pad, 0), padded(s_pad, 1)
        sums = (s_re * re + s_im * im, s_re * im - s_im * re)
        for c, at, own in spans():
            part[use, :, :, own, :] = sums[c].reshape(gx, gz, PAD, length)[:, :, 0:planes, at]
        order = nearest(gz)[::-1]
        for i, d in enumerate(order):
            for f in nearest(gx)[:0:-1]:
                to = along_x(f)
                remote(
                    part.at[use, to, along_z(d)], rx.at[use, x, i],
                    rsx_send.at[use], rsx_recv.at[use, x, i], device(y, to, z, h),
                ).start()
        hooks[0]()
        for i, d in enumerate(order):
            target = along_z(d)
            total = part[use, x, target]
            for f in nearest(gx)[1:]:
                source = along_x(f)
                got(rx.at[use, source, i], rsx_recv.at[use, source, i])
                total = total + rx[use, source, i]
            q[use, i] = total
            if d != 0:
                remote(
                    q.at[use, i], rz.at[use, z], rsz_send.at[use], rsz_recv.at[use, z],
                    device(y, x, target, h),
                ).start()
        hooks[1]()
        block = q[use, gz - 1]
        for d in nearest(gz)[1:]:
            source = along_z(d)
            got(rz.at[use, source], rsz_recv.at[use, source])
            block = block + rz[use, source]
        return block

    def start_gather(block, it):
        ag[it, x, z] = block
        mine = ag.at[it, x, z]
        for d in nearest(gz)[1:]:
            remote(
                mine, mine, agz_send.at[it], agz_recv.at[it, z], device(y, x, along_z(d), h)
            ).start()
        for k, (c, at, own) in enumerate(spans()):
            hz_send[it, 0, k : k + 1, :] = ag[it, x, z, own.start : own.start + 1, :]
            hz_send[it, 1, k : k + 1, :] = ag[it, x, z, own.stop - 1 : own.stop, :]
        for i, target in enumerate(((y, below), (y, above))):
            remote(
                hz_send.at[it, i], hz_recv.at[it, i], halo_send.at[it, i], halo_recv.at[it, i],
                target,
            ).start()
        for i, d in enumerate((gy - 1, 1)):
            remote(
                mine, hx_recv.at[it, i], halo_send.at[it, 2 + i], halo_recv.at[it, 2 + i],
                device(along_y(d), x, z, h),
            ).start()

    row_ids = lax.broadcasted_iota(jnp.int32, (PAD, length), 0)
    lane_ids = lax.broadcasted_iota(jnp.int32, (PAD, length), 1)

    def variation(it):
        for i in range(2):
            got(hz_recv.at[it, i], halo_recv.at[it, i])
            got(hx_recv.at[it, i], halo_recv.at[it, 2 + i])
        first = (slab > 0).astype(F32)
        last = (slab < slabs - 1).astype(F32)
        x_first = (y > 0).astype(F32)
        x_last = (y < gy - 1).astype(F32)
        for k, (c, at, own) in enumerate(spans()):
            frame[c, 1 : planes + 1, at] = ag[it, x, z, own, :]
            frame[c, planes + 1 : planes + 2, at] = hz_recv[it, 0, k : k + 1, :] * last
            frame[c, 0:1, at] = hz_recv[it, 1, k : k + 1, :] * first
            xframe[0, c, 1 : planes + 1, at] = hx_recv[it, 0, own, :] * x_last
            xframe[1, c, 1 : planes + 1, at] = hx_recv[it, 1, own, :] * x_first
        for c in range(2):
            v = frame[c]
            flux = wframe[0] * (pltpu.roll(v, PAD - 1, 0) - v)
            out = pltpu.roll(flux, 1, 0) - flux
            out = out + wframe[2] * (v - xframe[1, c]) - wframe[1] * (xframe[0, c] - v)
            ahead = jnp.where(lane_ids < length - 1, pltpu.roll(v, length - 1, 1), 0.0)
            flux = wframe[3] * (ahead - v)
            out = out + jnp.where(lane_ids > 0, pltpu.roll(flux, 1, 1), 0.0) - flux
            frame[c] = out
        for c, at, own in spans():
            smooth[it, own, :] = frame[c, 1 : planes + 1, at]

    def lanes(value):
        return jnp.sum(value, axis=0, keepdims=True)

    tile_rows = lax.broadcasted_iota(jnp.int32, ar_y.shape[2:], 0)

    def start_sums(values, it):
        tile = jnp.zeros(ar_y.shape[2:], F32)
        for i, value in enumerate(values):
            tile = jnp.where(tile_rows == i, value, tile)
        ar_y[it, y] = tile
        for d in range(1, gy):
            remote(
                ar_y.at[it, y], ar_y.at[it, y], ary_send.at[it], ary_recv.at[it, y],
                device(along_y(d), x, z, h),
            ).start()

    def total_of(slots, it, count):
        total = slots[it, 0]
        for i in range(1, count):
            total = total + slots[it, i]
        return total

    def sums_z(it):
        for d in range(1, gy):
            got(ar_y.at[it, along_y(d)], ary_recv.at[it, along_y(d)])
        ar_z[it, z] = total_of(ar_y, it, gy)
        for d in range(1, gz):
            remote(
                ar_z.at[it, z], ar_z.at[it, z], arz_send.at[it], arz_recv.at[it, z],
                device(y, x, along_z(d), h),
            ).start()

    def sums_x(it):
        for d in range(1, gz):
            got(ar_z.at[it, along_z(d)], arz_recv.at[it, along_z(d)])
        mine = x * 2 + h
        ar_x[it, mine] = total_of(ar_z, it, gz)
        for d in range(1, 2 * gx):
            to = (mine + d) % (2 * gx)
            remote(
                ar_x.at[it, mine], ar_x.at[it, mine], arx_send.at[it], arx_recv.at[it, mine],
                device(y, to // 2, z, to % 2),
            ).start()

    def finish_sums(it, count):
        mine = x * 2 + h
        for d in range(1, 2 * gx):
            source = (mine + d) % (2 * gx)
            got(ar_x.at[it, source], arx_recv.at[it, source])
        total = total_of(ar_x, it, 2 * gx)
        return [jnp.sum(jnp.where(tile_rows == i, total, 0.0)) for i in range(count)]

    def operator(block, it, sums):
        gather(ag.at[it], it)
        variation(it)
        unpack(v_pad, ag.at[it])
        v_re, v_im = padded(v_pad, 0), padded(v_pad, 1)
        s_re, s_im = padded(s_pad, 0), padded(s_pad, 1)
        coil = jnp.concatenate([s_re * v_re - s_im * v_im, s_re * v_im + s_im * v_re], axis=1)
        pieces = split(coil)
        if it == 0:
            table_copies[2].wait()
        t_send[it] = times_table(pieces, right, other)
        swap = remote(
            t_send.at[it], t_recv.at[it], core_send.at[3 + it], core_recv.at[3 + it], sibling
        )
        swap.start()
        mine = times_table(pieces, right, h)
        if it == 0:
            table_copies[3].wait()

        def left_of(value, which):
            tall = jnp.concatenate([value[:, 0:rows], value[:, rows : 2 * rows]], axis=0)
            return table_times(left, which, split(tall))

        spectrum = left_of(mine, h)
        swap.wait_recv()
        spectrum = spectrum + left_of(t_recv[it], other)
        spectrum = jnp.concatenate(
            [spectrum[0:length] * mask_t[...], spectrum[length : 2 * length] * mask_t[...]], axis=0
        )
        power = jnp.sum(spectrum * spectrum, axis=0, keepdims=True)
        folded = power[:, 0:width]
        for i in range(1, power.shape[1] // width):
            folded = folded + power[:, i * width : (i + 1) * width]
        start_sums([folded + lanes(block * smooth[it])] + sums, it)
        image = to_image(to_lines(spectrum, 1 + it), 1 + it)
        return coil_sum(image, 1 + it, (lambda: sums_z(it), lambda: sums_x(it))) + smooth[it]

    wframe[...] = jnp.zeros_like(wframe)
    frame[...] = jnp.zeros_like(frame)
    xframe[...] = jnp.zeros_like(xframe)
    got(wz_recv, w_recv.at[0])
    got(wx_recv, w_recv.at[1])
    wframe[0, 1 : planes + 1, :] = w_ref[0]
    wframe[0, 0:1, :] = wz_recv[0:1, :] * (slab > 0).astype(F32)
    wframe[1, 1 : planes + 1, :] = w_ref[1]
    wframe[2, 1 : planes + 1, :] = wx_recv[...] * (y > 0).astype(F32)
    wframe[3, 1 : planes + 1, :] = w_ref[2]

    for t in range(steps):
        over_z(t)
        if t + 2 < steps:
            sent(wy.at[t, pl.ds(0, gy - 1)], y_send.at[t])
            over_y(t + 2)
        if t > 0:
            over_x(t - 1)
        if t == 1:
            gather(mb, 2)
            for c, at, own in spans():
                if c == 0:
                    k_pad[0, :, 0:planes, at] = mb[:, :, own, :].reshape(chips, planes, width)
            mask_t[...] = padded(k_pad, 0).T
        if t == gx + 1:
            arrived(0)
            unpack(k_pad, kx)
            spectrum = jnp.concatenate([padded(k_pad, 0).T, padded(k_pad, 1).T], axis=0)
            lines = to_lines(spectrum, 0)
    over_x(steps - 1)
    image = to_image(lines, 0)
    arrived(1)
    unpack(s_pad, sx)
    first = coil_sum(image, 0, (lambda: None, lambda: None))

    start_gather(first, 0)
    applied = operator(first, 0, [lanes(first * first)])
    curvature, norm = finish_sums(0, 2)
    step = norm / curvature
    second = first - step * applied
    start_gather(second, 1)
    hold[0] = applied
    hold[1] = second
    fresh = operator(second, 1, [lanes(second * second), lanes(second * applied)])
    applied, second = hold[0], hold[1]
    first = ag[0, x, z]
    own, norm_next, cross = finish_sums(1, 3)
    ratio = norm_next / norm
    curvature_next = own + 2.0 * ratio * cross + ratio * ratio * curvature
    step_next = norm_next / curvature_next
    hold[0] = step * first + step_next * (second + ratio * first)
    hold[1] = second - step_next * (fresh + ratio * applied)
    for c, at, own in spans():
        x_out[c, :, at] = hold[0, own, :]
        r_out[c, :, at] = hold[1, own, :]

    for t in range(steps):
        if t + 2 >= steps:
            sent(wy.at[t, pl.ds(0, gy - 1)], y_send.at[t])
        sent(wz.at[t, pl.ds(0, gz - 1)], z_send.at[t])
        if t % gx != 0:
            sent(wz.at[t], x_send.at[t])
    for i in range(2):
        sent(ag.at[i, 0, pl.ds(0, gz - 1)], agz_send.at[i])
        sent(ag.at[i, pl.ds(0, gx - 1)], agx_send.at[i])
        sent(ar_y.at[i, pl.ds(0, gy - 1)], ary_send.at[i])
        sent(ar_z.at[i, pl.ds(0, gz - 1)], arz_send.at[i])
        sent(ar_x.at[i, pl.ds(0, 2 * gx - 1)], arx_send.at[i])
        sent(t_send.at[i], core_send.at[3 + i])
        for j in range(2):
            sent(hz_send.at[i, j], halo_send.at[i, j])
            sent(hx_recv.at[i, j], halo_send.at[i, 2 + j])
    for use in range(3):
        sent(rx.at[use, pl.ds(0, gx - 1)], rsx_send.at[use])
        sent(rz.at[use, pl.ds(0, gz - 1)], rsz_send.at[use])
        sent(u_send.at[use], core_send.at[use])
    sent(mb.at[0, pl.ds(0, gz - 1)], agz_send.at[2])
    sent(mb.at[pl.ds(0, gx - 1)], agx_send.at[2])
    sent(wz_send, w_send.at[0])
    sent(wx_recv, w_send.at[1])


def body(sizes, kspace, coil_maps, sampling, variation_weights):
    gx, gy, gz, planes, length, lanes = sizes
    chips = gx * gz
    rows = chips * PAD
    tiles = length // lanes
    sampled = sampling.astype(F32)

    def wired(array):
        parts, coils, _, positions, _ = array.shape
        shaped = array.reshape(parts, coils, planes, positions, tiles, lanes)
        return jnp.transpose(shaped, (3, 1, 0, 4, 2, 5)).reshape(positions, coils, -1, lanes)

    k_in = wired(kspace * sampled[None, None, :, None, :])
    s_in = wired(coil_maps.astype(F32))
    m_in = jnp.transpose(sampled.reshape(planes, tiles, lanes), (1, 0, 2)).reshape(-1, lanes)
    tables = fourier_tables(length, chips, planes)
    block = (2 * tiles * planes, lanes)
    rounds = (2 * gx, gy) + block
    last = (gx, gz) + block
    dma = pltpu.SemaphoreType.DMA
    vmem = pltpu.VMEM
    scratch = [vmem(table.shape, BF16) for table in tables]
    scratch += [vmem(shape, F32) for shape in (rounds, rounds, last, last)]
    scratch += [
        vmem((gx, gz, tiles * planes, lanes), F32),
        vmem((length, rows), F32),
        vmem((2, chips, PAD, length), F32),
        vmem((2, chips, PAD, length), F32),
        vmem((2, chips, PAD, length), F32),
        vmem((2, rows, 2 * rows), F32),
        vmem((2, rows, 2 * rows), F32),
        vmem((3, 2 * rows, rows), F32),
        vmem((3, 2 * rows, rows), F32),
        vmem((3,) + last, F32),
        vmem((3,) + last, F32),
        vmem((3, gz) + block, F32),
        vmem((3, gz) + block, F32),
        vmem((2,) + last, F32),
        vmem((PAD, length), F32),
        vmem((PAD, length), F32),
        vmem((planes, length), F32),
        vmem((2, 2, 2 * tiles, lanes), F32),
        vmem((2, 2, 2 * tiles, lanes), F32),
        vmem((2, 2) + block, F32),
        vmem((2, PAD, length), F32),
        vmem((2, 2, PAD, length), F32),
        vmem((4, PAD, length), F32),
        vmem((2,) + block, F32),
        vmem((2,) + block, F32),
        vmem((2, gy, 8, lanes), F32),
        vmem((2, gz, 8, lanes), F32),
        vmem((2, 2 * gx, 8, lanes), F32),
        dma((4,)),
        dma((2 * gx,)), dma((2 * gx,)), dma((2 * gx,)), dma((2 * gx,)), dma((2 * gx,)),
        dma((2 * gx,)),
        dma((3,)), dma((3, gz)), dma((3,)), dma((3,)),
        dma((3,)), dma((3, gx, gz)), dma((3,)), dma((3, gz)),
        dma((5,)), dma((5,)),
        dma((2,)), dma((2,)), dma((2, 4)), dma((2, 4)),
        dma((2,)), dma((2, gy)), dma((2,)), dma((2, gz)), dma((2,)), dma((2, 2 * gx)),
    ]
    in_vmem = pl.BlockSpec(memory_space=pltpu.VMEM)
    anywhere = pl.BlockSpec(memory_space=pl.ANY)
    image, residual = pl.pallas_call(
        partial(kernel, sizes),
        out_shape=[jax.ShapeDtypeStruct((2, planes, length), F32)] * 2,
        in_specs=[in_vmem] * 4 + [anywhere] * 4,
        out_specs=[in_vmem] * 2,
        scratch_shapes=scratch,
        compiler_params=pltpu.CompilerParams(
            collective_id=0, has_side_effects=True, vmem_limit_bytes=58 * 2**20
        ),
    )(k_in, s_in, m_in, variation_weights[:, :, 0, :], *[jnp.asarray(t) for t in tables])
    return image[:, :, None, :], residual[:, :, None, :]


def solution(mesh, gx=4, gz=8):
    gy = mesh.shape["coil"]

    def whole(kspace, coil_maps, sampling, variation_weights):
        length = kspace.shape[4]
        planes = length // (gx * gz * 2)
        sizes = (gx, gy, gz, planes, length, math.gcd(128, length, gx * gz * PAD))
        return jax.shard_map(
            partial(body, sizes),
            mesh=mesh,
            in_specs=(
                P(None, "coil", "slab", None, None),
                P(None, "coil", "slab", None, None),
                P("slab", None),
                P(None, "slab", "coil", None),
            ),
            out_specs=(P(None, "slab", "coil", None), P(None, "slab", "coil", None)),
            check_vma=False,
        )(kspace, coil_maps, sampling, variation_weights)

    return whole
```

```python
from functools import partial
import math

import jax
import jax.numpy as jnp
import numpy as np
from jax import lax
from jax.experimental import pallas as pl
from jax.experimental.pallas import tpu as pltpu
from jax.sharding import PartitionSpec as P

F32 = jnp.float32
BF16 = jnp.bfloat16
PAD = 8


def halves(table):
    high = table.astype(BF16)
    low = (table - high.astype(np.float32)).astype(BF16)
    return np.stack([high, low])


def fourier_tables(length, chips, planes):
    third = length // 3
    core, chip, plane = np.meshgrid(np.arange(2), np.arange(chips), np.arange(PAD), indexing="ij")
    owned = ((chip * 2 + core) * planes + plane).reshape(2, 1, -1)
    valid = (plane < planes).astype(np.float64).reshape(2, 1, -1) / math.sqrt(length)
    natural = np.arange(length, dtype=np.int64)
    angles = natural[None, :, None] * owned % length * (2.0 * math.pi / length)
    cosine, sine = np.cos(angles) * valid, np.sin(angles) * valid
    left = np.concatenate([cosine, sine], axis=2)
    back = np.concatenate([np.swapaxes(cosine, 1, 2), np.swapaxes(sine, 1, 2)], axis=2)
    right = []
    for r in range(3):
        columns = []
        for core in range(2):
            step, chip = np.meshgrid(np.arange(planes // 3), np.arange(chips), indexing="ij")
            lines = ((chip * 2 + core) * planes + 3 * step + r).reshape(1, -1)
            angles = np.arange(third)[:, None] * lines % length * (2.0 * math.pi / length)
            cosine, sine = np.cos(angles) / math.sqrt(length), np.sin(angles) / math.sqrt(length)
            columns.append(np.concatenate([cosine, sine], axis=0))
            columns.append(np.concatenate([-sine, cosine], axis=0))
        right.append(np.concatenate(columns, axis=1))
    right = np.stack(right)
    home = np.swapaxes(right, 1, 2)
    return tuple(halves(table.astype(np.float32)) for table in (right, left, back, home))


def thirds(parts, orient):
    (re0, im0), (re1, im1), (re2, im2) = parts
    turn = orient * math.sqrt(0.75)
    sum_re, sum_im = re1 + re2, im1 + im2
    dif_re, dif_im = turn * (re1 - re2), turn * (im1 - im2)
    mid_re, mid_im = re0 - 0.5 * sum_re, im0 - 0.5 * sum_im
    return (
        (re0 + sum_re, im0 + sum_im),
        (mid_re + dif_im, mid_im - dif_re),
        (mid_re - dif_im, mid_im + dif_re),
    )


def split(value):
    high = value.astype(BF16)
    return high, (value - high.astype(F32)).astype(BF16)


def dot(a, b):
    return jnp.dot(a, b, preferred_element_type=F32)


def times_table(value, table, which):
    high, low = value
    return (
        dot(high, table[0, which]) + dot(low, table[0, which]) + dot(high, table[1, which])
    )


def table_times(table, which, value):
    high, low = value
    return (
        dot(table[0, which], high) + dot(table[0, which], low) + dot(table[1, which], high)
    )


def nearest(count):
    offsets = [0]
    for d in range(1, count // 2):
        offsets += [d, -d]
    return offsets + [count // 2]


def kernel(
    sizes,
    k_ref, s_ref, m_ref, w_ref, right_hbm, left_hbm, back_hbm, home_hbm,
    x_out, r_out,
    right, left, back, home,
    wy, wz, kx, sx, mb,
    mask_t, s_pad, v_pad, k_pad,
    t_pair, t_recv, u_send, u_pair,
    part, rx, q, rz, ag,
    wz_send, wz_recv, wx_recv, hz_send, hz_recv, hx_recv,
    frame, xframe, wframe, smooth, hold,
    ar_y, ar_z, ar_x,
    table_sem,
    y_send, y_recv, z_send, z_recv, x_send, x_recv,
    agz_send, agz_recv, agx_send, agx_recv,
    rsx_send, rsx_recv, rsz_send, rsz_recv,
    core_send, core_recv,
    w_send, w_recv, halo_send, halo_recv,
    ary_send, ary_recv, arz_send, arz_recv, arx_send, arx_recv,
):
    gx, gy, gz, planes, length, width = sizes
    chips = gx * gz
    rows = chips * PAD
    tiles = length // width
    third = length // 3
    pair = 2 * (planes // 3) * chips
    y = lax.axis_index("coil")
    slab = lax.axis_index("slab")
    x = slab // (gz * 2)
    z = (slab // 2) % gz
    h = slab % 2
    other = 1 - h

    def device(y_, x_, z_, h_):
        return (y_, (x_ * gz + z_) * 2 + h_)

    def remote(src, dst, send_sem, recv_sem, target):
        return pltpu.make_async_remote_copy(
            src_ref=src, dst_ref=dst, send_sem=send_sem, recv_sem=recv_sem,
            device_id=target, device_id_type=pl.DeviceIdType.MESH,
        )

    sibling = device(y, x, z, other)

    def got(dst, recv_sem):
        remote(dst, dst, recv_sem, recv_sem, sibling).wait_recv()

    def sent(src, send_sem):
        remote(src, src, send_sem, send_sem, sibling).wait_send()

    def along_y(d):
        return (y + d + gy) % gy

    def along_z(d):
        return (z + d + gz) % gz

    def along_x(d):
        return (x + d + gx) % gx

    table_copies = [
        pltpu.make_async_copy(src, dst, table_sem.at[i])
        for i, (src, dst) in enumerate(
            ((back_hbm, back), (home_hbm, home), (right_hbm, right), (left_hbm, left))
        )
    ]
    for copy in table_copies:
        copy.start()

    slabs = gx * gz * 2
    below = (slab + slabs - 1) % slabs
    above = (slab + 1) % slabs
    barrier = pltpu.get_barrier_semaphore()

    def greet(target):
        pl.semaphore_signal(barrier, inc=1, device_id=target, device_id_type=pl.DeviceIdType.MESH)

    for d in range(1, gy):
        greet(device(along_y(d), x, z, h))
    for d in range(1, gz):
        greet(device(y, x, along_z(d), h))
    for d in range(1, gx):
        greet(device(y, along_x(d), z, h))
        greet(device(y, along_x(d), z, other))
    greet(sibling)
    greet((y, jnp.where(h == 0, below, above)))
    pl.semaphore_wait(barrier, (gy - 1) + (gz - 1) + 2 * (gx - 1) + 2)

    steps = 2 * gx
    sources = (k_ref, s_ref)
    ends = (kx, sx)

    def over_y(t):
        source, coil = sources[t // gx], along_x(t % gx)
        for d in nearest(gy)[:0:-1]:
            to = along_y(d)
            remote(
                source.at[to, coil], wy.at[t, y], y_send.at[t], y_recv.at[t], device(to, x, z, h)
            ).start()
        wy[t, y] = source[y, coil]

    def over_z(t):
        got(wy.at[t, pl.ds(0, gy - 1)], y_recv.at[t])
        for d in nearest(gz)[:0:-1]:
            to = along_z(d)
            remote(
                wy.at[t, to], wz.at[t, z], z_send.at[t], z_recv.at[t], device(y, x, to, h)
            ).start()
        wz[t, z] = wy[t, z]

    def over_x(t):
        got(wz.at[t, pl.ds(0, gz - 1)], z_recv.at[t])
        end = ends[t // gx]
        if t % gx == 0:
            end[x] = wz[t]
        else:
            remote(
                wz.at[t], end.at[x], x_send.at[t], x_recv.at[t],
                device(y, along_x(t % gx), z, h),
            ).start()

    def arrived(i):
        for f in range(1, gx):
            got(ends[i].at[along_x(gx - f)], x_recv.at[i * gx + f])

    over_y(0)
    over_y(1)

    lines = m_ref[...].astype(F32)
    for i in range(tiles):
        mb[x, z, i * planes : (i + 1) * planes, :] = lines[:, i * width : (i + 1) * width]
    for d in nearest(gz)[1:]:
        remote(
            mb.at[x, z], mb.at[x, z], agz_send.at[2], agz_recv.at[2, z],
            device(y, x, along_z(d), h),
        ).start()
    wz_send[0:1, :] = w_ref[0, planes - 1, :, :]
    remote(wz_send, wz_recv, w_send.at[0], w_recv.at[0], (y, above)).start()
    remote(w_ref.at[1], wx_recv, w_send.at[1], w_recv.at[1], device(along_y(1), x, z, h)).start()

    s_pad[...] = jnp.zeros_like(s_pad)
    v_pad[...] = jnp.zeros_like(v_pad)

    def gather(slots, use):
        for d in nearest(gz):
            block = slots.at[x, along_z(d)]
            if d != 0:
                got(block, agz_recv.at[use, along_z(d)])
            for f in nearest(gx)[:0:-1]:
                remote(
                    block, block, agx_send.at[use], agx_recv.at[use],
                    device(y, along_x(f), z, h),
                ).start()
    def gathered(slots, use):
        got(slots.at[pl.ds(0, gx - 1)], agx_recv.at[use])

    def spans():
        for c in range(2):
            for i in range(tiles):
                first = (c * tiles + i) * planes
                yield c, slice(i * width, (i + 1) * width), slice(first, first + planes)

    def unpack(pad, blocks):
        for c, at, own in spans():
            pad[c, :, 0:planes, at] = blocks[:, :, own, :].reshape(chips, planes, width)

    def padded(ref, index):
        return ref[index].reshape(rows, length)

    lane_sign = jnp.where(
        lax.broadcasted_iota(jnp.int32, (1, pair), 1) < pair // 2, 1.0, -1.0
    ).astype(F32)

    def group(value, r):
        return value[:, r * pair : (r + 1) * pair]

    def with_turned(value, sign):
        turned = [
            pltpu.roll(group(value, r), pair // 2, 1) * (sign * lane_sign) for r in range(3)
        ]
        return split(jnp.concatenate([value, jnp.concatenate(turned, axis=1)], axis=0))

    def to_lines(spectrum, use):
        pieces = with_turned(spectrum, -1.0)
        if use == 0:
            table_copies[0].wait()
        u_send[use] = table_times(back, other, pieces)
        remote(
            u_send.at[use], u_pair.at[use, h], core_send.at[use], core_recv.at[use], sibling
        ).start()
        u_pair[use, h] = table_times(back, h, pieces)

    def to_image(use):
        if use == 0:
            table_copies[1].wait()
        got(u_pair.at[use, other], core_recv.at[use])
        first, second = u_pair[use, 0], u_pair[use, 1]
        parts = []
        for r in range(3):
            wide = jnp.concatenate([group(first, r), group(second, r)], axis=1)
            product = times_table(split(wide), home, r)
            parts.append((product[:, 0:third], product[:, third : 2 * third]))
        parts = thirds(parts, -1.0)
        return [jnp.concatenate([part[c] for part in parts], axis=1) for c in range(2)]

    def coil_sum(image, use, hooks):
        re, im = image
        s_re, s_im = padded(s_pad, 0), padded(s_pad, 1)
        sums = (s_re * re + s_im * im, s_re * im - s_im * re)
        for c, at, own in spans():
            part[use, :, :, own, :] = sums[c].reshape(gx, gz, PAD, length)[:, :, 0:planes, at]
        order = nearest(gz)[::-1]
        for i, d in enumerate(order):
            for f in nearest(gx)[:0:-1]:
                to = along_x(f)
                remote(
                    part.at[use, to, along_z(d)], rx.at[use, x, i],
                    rsx_send.at[use], rsx_recv.at[use, x, i], device(y, to, z, h),
                ).start()
        hooks[0]()
        for i, d in enumerate(order):
            target = along_z(d)
            total = part[use, x, target]
            for f in nearest(gx)[1:]:
                source = along_x(f)
                got(rx.at[use, source, i], rsx_recv.at[use, source, i])
                total = total + rx[use, source, i]
            q[use, i] = total
            if d != 0:
                remote(
                    q.at[use, i], rz.at[use, z], rsz_send.at[use], rsz_recv.at[use, z],
                    device(y, x, target, h),
                ).start()
        hooks[1]()
        block = q[use, gz - 1]
        for d in nearest(gz)[1:]:
            source = along_z(d)
            got(rz.at[use, source], rsz_recv.at[use, source])
            block = block + rz[use, source]
        return block

    def start_gather(block, it):
        ag[it, x, z] = block
        mine = ag.at[it, x, z]
        for d in nearest(gz)[1:]:
            remote(
                mine, mine, agz_send.at[it], agz_recv.at[it, z], device(y, x, along_z(d), h)
            ).start()
        for k, (c, at, own) in enumerate(spans()):
            hz_send[it, 0, k : k + 1, :] = ag[it, x, z, own.start : own.start + 1, :]
            hz_send[it, 1, k : k + 1, :] = ag[it, x, z, own.stop - 1 : own.stop, :]
        for i, target in enumerate(((y, below), (y, above))):
            remote(
                hz_send.at[it, i], hz_recv.at[it, i], halo_send.at[it, i], halo_recv.at[it, i],
                target,
            ).start()
        for i, d in enumerate((gy - 1, 1)):
            remote(
                mine, hx_recv.at[it, i], halo_send.at[it, 2 + i], halo_recv.at[it, 2 + i],
                device(along_y(d), x, z, h),
            ).start()

    row_ids = lax.broadcasted_iota(jnp.int32, (PAD, length), 0)
    lane_ids = lax.broadcasted_iota(jnp.int32, (PAD, length), 1)

    def variation(it):
        for i in range(2):
            got(hz_recv.at[it, i], halo_recv.at[it, i])
            got(hx_recv.at[it, i], halo_recv.at[it, 2 + i])
        first = (slab > 0).astype(F32)
        last = (slab < slabs - 1).astype(F32)
        x_first = (y > 0).astype(F32)
        x_last = (y < gy - 1).astype(F32)
        for k, (c, at, own) in enumerate(spans()):
            frame[c, 1 : planes + 1, at] = ag[it, x, z, own, :]
            frame[c, planes + 1 : planes + 2, at] = hz_recv[it, 0, k : k + 1, :] * last
            frame[c, 0:1, at] = hz_recv[it, 1, k : k + 1, :] * first
            xframe[0, c, 1 : planes + 1, at] = hx_recv[it, 0, own, :] * x_last
            xframe[1, c, 1 : planes + 1, at] = hx_recv[it, 1, own, :] * x_first
        for c in range(2):
            v = frame[c]
            flux = wframe[0] * (pltpu.roll(v, PAD - 1, 0) - v)
            out = pltpu.roll(flux, 1, 0) - flux
            out = out + wframe[2] * (v - xframe[1, c]) - wframe[1] * (xframe[0, c] - v)
            ahead = jnp.where(lane_ids < length - 1, pltpu.roll(v, length - 1, 1), 0.0)
            flux = wframe[3] * (ahead - v)
            out = out + jnp.where(lane_ids > 0, pltpu.roll(flux, 1, 1), 0.0) - flux
            frame[c] = out
        for c, at, own in spans():
            smooth[it, own, :] = frame[c, 1 : planes + 1, at]

    def lanes(value):
        return jnp.sum(value, axis=0, keepdims=True)

    tile_rows = lax.broadcasted_iota(jnp.int32, ar_y.shape[2:], 0)

    def start_sums(values, it):
        tile = jnp.zeros(ar_y.shape[2:], F32)
        for i, value in enumerate(values):
            tile = jnp.where(tile_rows == i, value, tile)
        ar_y[it, y] = tile
        for d in range(1, gy):
            remote(
                ar_y.at[it, y], ar_y.at[it, y], ary_send.at[it], ary_recv.at[it, y],
                device(along_y(d), x, z, h),
            ).start()

    def total_of(slots, it, count):
        total = slots[it, 0]
        for i in range(1, count):
            total = total + slots[it, i]
        return total

    def sums_z(it):
        for d in range(1, gy):
            got(ar_y.at[it, along_y(d)], ary_recv.at[it, along_y(d)])
        ar_z[it, z] = total_of(ar_y, it, gy)
        for d in range(1, gz):
            remote(
                ar_z.at[it, z], ar_z.at[it, z], arz_send.at[it], arz_recv.at[it, z],
                device(y, x, along_z(d), h),
            ).start()

    def sums_x(it):
        for d in range(1, gz):
            got(ar_z.at[it, along_z(d)], arz_recv.at[it, along_z(d)])
        mine = x * 2 + h
        ar_x[it, mine] = total_of(ar_z, it, gz)
        for d in range(1, 2 * gx):
            to = (mine + d) % (2 * gx)
            remote(
                ar_x.at[it, mine], ar_x.at[it, mine], arx_send.at[it], arx_recv.at[it, mine],
                device(y, to // 2, z, to % 2),
            ).start()

    def finish_sums(it, count):
        mine = x * 2 + h
        for d in range(1, 2 * gx):
            source = (mine + d) % (2 * gx)
            got(ar_x.at[it, source], arx_recv.at[it, source])
        total = total_of(ar_x, it, 2 * gx)
        return [jnp.sum(jnp.where(tile_rows == i, total, 0.0)) for i in range(count)]

    def operator(block, it, sums):
        gather(ag.at[it], it)
        variation(it)
        gathered(ag.at[it], it)
        unpack(v_pad, ag.at[it])
        v_re, v_im = padded(v_pad, 0), padded(v_pad, 1)
        s_re, s_im = padded(s_pad, 0), padded(s_pad, 1)
        coil_re, coil_im = s_re * v_re - s_im * v_im, s_re * v_im + s_im * v_re
        parts = thirds(
            [
                (coil_re[:, a * third : (a + 1) * third], coil_im[:, a * third : (a + 1) * third])
                for a in range(3)
            ],
            1.0,
        )
        if it == 0:
            table_copies[2].wait()
        for r in range(3):
            product = times_table(split(jnp.concatenate(parts[r], axis=1)), right, r)
            for core in range(2):
                t_pair[it, core, :, r * pair : (r + 1) * pair] = group(product, core)
        swap = remote(
            t_pair.at[it, other], t_recv.at[it], core_send.at[3 + it], core_recv.at[3 + it],
            sibling,
        )
        swap.start()
        if it == 0:
            table_copies[3].wait()
        spectrum = table_times(left, h, with_turned(t_pair[it, h], 1.0))
        swap.wait_recv()
        spectrum = spectrum + table_times(left, other, with_turned(t_recv[it], 1.0))
        spectrum = spectrum * mask_t[...]
        power = jnp.sum(spectrum * spectrum, axis=0, keepdims=True)
        folded = power[:, 0:width]
        for i in range(1, power.shape[1] // width):
            folded = folded + power[:, i * width : (i + 1) * width]
        start_sums([folded + lanes(block * smooth[it])] + sums, it)
        to_lines(spectrum, 1 + it)
        image = to_image(1 + it)
        return coil_sum(image, 1 + it, (lambda: sums_z(it), lambda: sums_x(it))) + smooth[it]

    wframe[...] = jnp.zeros_like(wframe)
    frame[...] = jnp.zeros_like(frame)
    xframe[...] = jnp.zeros_like(xframe)
    got(wz_recv, w_recv.at[0])
    got(wx_recv, w_recv.at[1])
    wframe[0, 1 : planes + 1, :] = w_ref[0, :, 0, :]
    wframe[0, 0:1, :] = wz_recv[0:1, :] * (slab > 0).astype(F32)
    wframe[1, 1 : planes + 1, :] = w_ref[1, :, 0, :]
    wframe[2, 1 : planes + 1, :] = wx_recv[:, 0, :] * (y > 0).astype(F32)
    wframe[3, 1 : planes + 1, :] = w_ref[2, :, 0, :]

    for t in range(steps):
        over_z(t)
        if t + 2 < steps:
            sent(wy.at[t, pl.ds(0, gy - 1)], y_send.at[t])
            over_y(t + 2)
        if t > 0:
            over_x(t - 1)
        if t == 1:
            gather(mb, 2)

    def unpack_lines(blocks, both):
        for c, at, own in spans():
            for j in range(planes):
                row = (j % 3) * pair + c * (pair // 2) + (j // 3) * chips
                k = own.start + j - (c * tiles * planes if both else 0)
                k_pad[row : row + chips, at] = blocks[:, :, k, :].reshape(chips, width)
        return k_pad[...].T

    gathered(mb, 2)
    mask_t[...] = unpack_lines(mb, True)
    arrived(0)
    to_lines(unpack_lines(kx, False), 0)
    over_x(steps - 1)
    image = to_image(0)
    arrived(1)
    unpack(s_pad, sx)
    first = coil_sum(image, 0, (lambda: None, lambda: None))

    start_gather(first, 0)
    applied = operator(first, 0, [lanes(first * first)])
    curvature, norm = finish_sums(0, 2)
    step = norm / curvature
    second = first - step * applied
    start_gather(second, 1)
    hold[0] = applied
    hold[1] = second
    fresh = operator(second, 1, [lanes(second * second), lanes(second * applied)])
    applied, second = hold[0], hold[1]
    first = ag[0, x, z]
    own, norm_next, cross = finish_sums(1, 3)
    ratio = norm_next / norm
    curvature_next = own + 2.0 * ratio * cross + ratio * ratio * curvature
    step_next = norm_next / curvature_next
    hold[0] = step * first + step_next * (second + ratio * first)
    hold[1] = second - step_next * (fresh + ratio * applied)
    for c, at, own in spans():
        x_out[c, :, at] = hold[0, own, :]
        r_out[c, :, at] = hold[1, own, :]

    for t in range(steps):
        if t + 2 >= steps:
            sent(wy.at[t, pl.ds(0, gy - 1)], y_send.at[t])
        sent(wz.at[t, pl.ds(0, gz - 1)], z_send.at[t])
        if t % gx != 0:
            sent(wz.at[t], x_send.at[t])
    for i in range(2):
        sent(ag.at[i, 0, pl.ds(0, gz - 1)], agz_send.at[i])
        sent(ag.at[i, pl.ds(0, gx - 1)], agx_send.at[i])
        sent(ar_y.at[i, pl.ds(0, gy - 1)], ary_send.at[i])
        sent(ar_z.at[i, pl.ds(0, gz - 1)], arz_send.at[i])
        sent(ar_x.at[i, pl.ds(0, 2 * gx - 1)], arx_send.at[i])
        sent(t_recv.at[i], core_send.at[3 + i])
        for j in range(2):
            sent(hz_send.at[i, j], halo_send.at[i, j])
            sent(hx_recv.at[i, j], halo_send.at[i, 2 + j])
    for use in range(3):
        sent(rx.at[use, pl.ds(0, gx - 1)], rsx_send.at[use])
        sent(rz.at[use, pl.ds(0, gz - 1)], rsz_send.at[use])
        sent(u_send.at[use], core_send.at[use])
    sent(mb.at[0, pl.ds(0, gz - 1)], agz_send.at[2])
    sent(mb.at[pl.ds(0, gx - 1)], agx_send.at[2])
    sent(wz_send, w_send.at[0])
    sent(wx_recv, w_send.at[1])


def body(sizes, kspace, coil_maps, sampling, variation_weights):
    gx, gy, gz, planes, length, lanes = sizes
    chips = gx * gz
    rows = chips * PAD
    tiles = length // lanes
    sampled = sampling.astype(F32)

    def wired(array):
        parts, coils, _, positions, _ = array.shape
        shaped = array.reshape(parts, coils, planes, positions, tiles, lanes)
        return jnp.transpose(shaped, (3, 1, 0, 4, 2, 5)).reshape(positions, coils, -1, lanes)

    k_in = wired(kspace * sampled[None, None, :, None, :])
    s_in = wired(coil_maps.astype(F32))
    tables = fourier_tables(length, chips, planes)
    block = (2 * tiles * planes, lanes)
    rounds = (2 * gx, gy) + block
    last = (gx, gz) + block
    dma = pltpu.SemaphoreType.DMA
    vmem = pltpu.VMEM
    scratch = [vmem(table.shape, BF16) for table in tables]
    scratch += [vmem(shape, F32) for shape in (rounds, rounds, last, last)]
    scratch += [
        vmem((gx, gz, tiles * planes, lanes), F32),
        vmem((length, length), F32),
        vmem((2, chips, PAD, length), F32),
        vmem((2, chips, PAD, length), F32),
        vmem((length, length), F32),
        vmem((2, 2, rows, length), F32),
        vmem((2, rows, length), F32),
        vmem((3, rows, length), F32),
        vmem((3, 2, rows, length), F32),
        vmem((3,) + last, F32),
        vmem((3,) + last, F32),
        vmem((3, gz) + block, F32),
        vmem((3, gz) + block, F32),
        vmem((2,) + last, F32),
        vmem((PAD, length), F32),
        vmem((PAD, length), F32),
        vmem((planes, 1, length), F32),
        vmem((2, 2, 2 * tiles, lanes), F32),
        vmem((2, 2, 2 * tiles, lanes), F32),
        vmem((2, 2) + block, F32),
        vmem((2, PAD, length), F32),
        vmem((2, 2, PAD, length), F32),
        vmem((4, PAD, length), F32),
        vmem((2,) + block, F32),
        vmem((2,) + block, F32),
        vmem((2, gy, 8, lanes), F32),
        vmem((2, gz, 8, lanes), F32),
        vmem((2, 2 * gx, 8, lanes), F32),
        dma((4,)),
        dma((2 * gx,)), dma((2 * gx,)), dma((2 * gx,)), dma((2 * gx,)), dma((2 * gx,)),
        dma((2 * gx,)),
        dma((3,)), dma((3, gz)), dma((3,)), dma((3,)),
        dma((3,)), dma((3, gx, gz)), dma((3,)), dma((3, gz)),
        dma((5,)), dma((5,)),
        dma((2,)), dma((2,)), dma((2, 4)), dma((2, 4)),
        dma((2,)), dma((2, gy)), dma((2,)), dma((2, gz)), dma((2,)), dma((2, 2 * gx)),
    ]
    in_vmem = pl.BlockSpec(memory_space=pltpu.VMEM)
    anywhere = pl.BlockSpec(memory_space=pl.ANY)
    image, residual = pl.pallas_call(
        partial(kernel, sizes),
        out_shape=[jax.ShapeDtypeStruct((2, planes, length), F32)] * 2,
        in_specs=[in_vmem] * 4 + [anywhere] * 4,
        out_specs=[in_vmem] * 2,
        scratch_shapes=scratch,
        compiler_params=pltpu.CompilerParams(
            collective_id=0, has_side_effects=True, vmem_limit_bytes=58 * 2**20
        ),
    )(k_in, s_in, sampling, variation_weights, *[jnp.asarray(t) for t in tables])
    return image[:, :, None, :], residual[:, :, None, :]


def solution(mesh, gx=4, gz=8):
    gy = mesh.shape["coil"]

    def whole(kspace, coil_maps, sampling, variation_weights):
        length = kspace.shape[4]
        planes = length // (gx * gz * 2)
        sizes = (gx, gy, gz, planes, length, math.gcd(128, length, gx * gz * PAD))
        return jax.shard_map(
            partial(body, sizes),
            mesh=mesh,
            in_specs=(
                P(None, "coil", "slab", None, None),
                P(None, "coil", "slab", None, None),
                P("slab", None),
                P(None, "slab", "coil", None),
            ),
            out_specs=(P(None, "slab", "coil", None), P(None, "slab", "coil", None)),
            check_vma=False,
        )(kspace, coil_maps, sampling, variation_weights)

    return whole
```

```python
from functools import partial
import math

import jax
import jax.numpy as jnp
import numpy as np
from jax import lax
from jax.experimental import pallas as pl
from jax.experimental.pallas import tpu as pltpu
from jax.sharding import PartitionSpec as P

F32 = jnp.float32
BF16 = jnp.bfloat16
PAD = 8


def halves(table):
    high = table.astype(BF16)
    low = (table - high.astype(np.float32)).astype(BF16)
    return np.stack([high, low])


def fourier_tables(length, chips, planes):
    third = length // 3
    core, chip, plane = np.meshgrid(np.arange(2), np.arange(chips), np.arange(PAD), indexing="ij")
    owned = ((chip * 2 + core) * planes + plane).reshape(2, 1, -1)
    valid = (plane < planes).astype(np.float64).reshape(2, 1, -1) / math.sqrt(length)
    natural = np.arange(length, dtype=np.int64)
    angles = natural[None, :, None] * owned % length * (2.0 * math.pi / length)
    cosine, sine = np.cos(angles) * valid, np.sin(angles) * valid
    left = np.concatenate([cosine, sine], axis=2)
    back = np.concatenate([np.swapaxes(cosine, 1, 2), np.swapaxes(sine, 1, 2)], axis=2)
    right = []
    for r in range(3):
        columns = []
        for core in range(2):
            step, chip = np.meshgrid(np.arange(planes // 3), np.arange(chips), indexing="ij")
            lines = ((chip * 2 + core) * planes + 3 * step + r).reshape(1, -1)
            angles = np.arange(third)[:, None] * lines % length * (2.0 * math.pi / length)
            cosine, sine = np.cos(angles) / math.sqrt(length), np.sin(angles) / math.sqrt(length)
            columns.append(np.concatenate([cosine, sine], axis=0))
            columns.append(np.concatenate([-sine, cosine], axis=0))
        right.append(np.concatenate(columns, axis=1))
    right = np.stack(right)
    home = np.swapaxes(right, 1, 2)
    return tuple(halves(table.astype(np.float32)) for table in (right, left, back, home))


def thirds(parts, orient):
    (re0, im0), (re1, im1), (re2, im2) = parts
    turn = orient * math.sqrt(0.75)
    sum_re, sum_im = re1 + re2, im1 + im2
    dif_re, dif_im = turn * (re1 - re2), turn * (im1 - im2)
    mid_re, mid_im = re0 - 0.5 * sum_re, im0 - 0.5 * sum_im
    return (
        (re0 + sum_re, im0 + sum_im),
        (mid_re + dif_im, mid_im - dif_re),
        (mid_re - dif_im, mid_im + dif_re),
    )


def split(value):
    high = value.astype(BF16)
    return high, (value - high.astype(F32)).astype(BF16)


def dot(a, b):
    return jnp.dot(a, b, preferred_element_type=F32)


def times_table(value, table, which):
    high, low = value
    return (
        dot(high, table[0, which]) + dot(low, table[0, which]) + dot(high, table[1, which])
    )


def table_times(table, which, value):
    high, low = value
    return (
        dot(table[0, which], high) + dot(table[0, which], low) + dot(table[1, which], high)
    )


def nearest(count):
    offsets = [0]
    for d in range(1, count // 2):
        offsets += [d, -d]
    return offsets + [count // 2]


def kernel(
    sizes,
    k_hbm, s_raw, m_ref, w_ref, right_hbm, left_hbm, back_hbm, home_hbm,
    x_out, r_out,
    right, left, back, home,
    k_raw, stage, k_ref, s_ref,
    wy, wz, kx, sx, mb,
    mask_t, s_pad, v_pad, k_pad,
    t_pair, t_recv, u_send, u_pair,
    part, rx, q, rz, ag,
    wz_send, wz_recv, wx_recv, hz_send, hz_recv, hx_recv,
    frame, xframe, wframe, smooth, hold, early,
    ar_y, ar_z, ar_x,
    table_sem, k_sem,
    y_send, y_recv, z_send, z_recv, x_send, x_recv,
    agz_send, agz_recv, agx_send, agx_recv,
    rsx_send, rsx_recv, rsz_send, rsz_recv,
    core_send, core_recv, swap_send, swap_recv,
    w_send, w_recv, halo_send, halo_recv,
    ary_send, ary_recv, arz_send, arz_recv, arx_send, arx_recv,
):
    gx, gy, gz, planes, length, width = sizes
    chips = gx * gz
    rows = chips * PAD
    tiles = length // width
    third = length // 3
    pair = 2 * (planes // 3) * chips
    y = lax.axis_index("coil")
    slab = lax.axis_index("slab")
    x = slab // (gz * 2)
    z = (slab // 2) % gz
    h = slab % 2
    other = 1 - h

    def device(y_, x_, z_, h_):
        return (y_, (x_ * gz + z_) * 2 + h_)

    def remote(src, dst, send_sem, recv_sem, target):
        return pltpu.make_async_remote_copy(
            src_ref=src, dst_ref=dst, send_sem=send_sem, recv_sem=recv_sem,
            device_id=target, device_id_type=pl.DeviceIdType.MESH,
        )

    sibling = device(y, x, z, other)

    def got(dst, recv_sem):
        remote(dst, dst, recv_sem, recv_sem, sibling).wait_recv()

    def sent(src, send_sem):
        remote(src, src, send_sem, send_sem, sibling).wait_send()

    def along_y(d):
        return (y + d + gy) % gy

    def along_z(d):
        return (z + d + gz) % gz

    def along_x(d):
        return (x + d + gx) % gx

    k_copy = pltpu.make_async_copy(k_hbm, k_raw, k_sem)
    k_copy.start()
    table_copies = [
        pltpu.make_async_copy(src, dst, table_sem.at[i])
        for i, (src, dst) in enumerate(
            ((back_hbm, back), (home_hbm, home), (right_hbm, right), (left_hbm, left))
        )
    ]
    for copy in table_copies:
        copy.start()

    slabs = gx * gz * 2
    below = (slab + slabs - 1) % slabs
    above = (slab + 1) % slabs
    barrier = pltpu.get_barrier_semaphore()

    def greet(target):
        pl.semaphore_signal(barrier, inc=1, device_id=target, device_id_type=pl.DeviceIdType.MESH)

    for d in range(1, gy):
        greet(device(along_y(d), x, z, h))
    for d in range(1, gz):
        greet(device(y, x, along_z(d), h))
    for d in range(1, gx):
        greet(device(y, along_x(d), z, h))
        greet(device(y, along_x(d), z, other))
    greet(sibling)
    greet((y, jnp.where(h == 0, below, above)))
    for ref in (s_pad, v_pad, frame, xframe, wframe):
        ref[...] = jnp.zeros_like(ref)
    lines = m_ref[...].astype(F32)
    for i in range(tiles):
        mb[x, z, i * planes : (i + 1) * planes, :] = lines[:, i * width : (i + 1) * width]
    wz_send[0:1, :] = w_ref[0, planes - 1, :, :]

    def by_position(value_of, wires):
        for coil in range(gx):
            for c in range(2):
                value = value_of(c, coil).reshape(planes * gy, length)
                for i in range(tiles):
                    first = (c * tiles + i) * planes
                    stage[c, coil, i] = value[:, i * width : (i + 1) * width]
                    for to in range(gy):
                        wires[to, coil, first : first + planes, :] = stage[
                            c, coil, i, pl.ds(to, planes, stride=gy), :
                        ]

    k_copy.wait()
    by_position(lambda c, coil: k_raw[c, coil] * lines[:, None, :], k_ref)
    pl.semaphore_wait(barrier, (gy - 1) + (gz - 1) + 2 * (gx - 1) + 2)

    steps = 2 * gx
    sources = (k_ref, s_ref)
    ends = (kx, sx)

    def over_y(t):
        source, coil = sources[t // gx], along_x((t + 1) % gx)
        for d in nearest(gy)[:0:-1]:
            to = along_y(d)
            remote(
                source.at[to, coil], wy.at[t, y], y_send.at[t], y_recv.at[t], device(to, x, z, h)
            ).start()
        wy[t, y] = source[y, coil]

    def over_z(t):
        got(wy.at[t, pl.ds(0, gy - 1)], y_recv.at[t])
        for d in nearest(gz)[:0:-1]:
            to = along_z(d)
            remote(
                wy.at[t, to], wz.at[t, z], z_send.at[t], z_recv.at[t], device(y, x, to, h)
            ).start()
        wz[t, z] = wy[t, z]

    def over_x(t):
        got(wz.at[t, pl.ds(0, gz - 1)], z_recv.at[t])
        end = ends[t // gx]
        if (t + 1) % gx == 0:
            end[x] = wz[t]
        else:
            remote(
                wz.at[t], end.at[x], x_send.at[t], x_recv.at[t],
                device(y, along_x((t + 1) % gx), z, h),
            ).start()

    def arrived(i):
        for f in range(1, gx):
            got(ends[i].at[along_x(gx - f)], x_recv.at[i * gx + f - 1])

    over_y(0)
    over_y(1)
    by_position(lambda c, coil: s_raw[c, coil].astype(F32), s_ref)

    for d in nearest(gz)[1:]:
        remote(
            mb.at[x, z], mb.at[x, z], agz_send.at[2], agz_recv.at[2, z],
            device(y, x, along_z(d), h),
        ).start()
    remote(wz_send, wz_recv, w_send.at[0], w_recv.at[0], (y, above)).start()
    remote(w_ref.at[1], wx_recv, w_send.at[1], w_recv.at[1], device(along_y(1), x, z, h)).start()

    def gather(slots, use):
        for d in nearest(gz):
            block = slots.at[x, along_z(d)]
            if d != 0:
                got(block, agz_recv.at[use, along_z(d)])
            for f in nearest(gx)[:0:-1]:
                remote(
                    block, block, agx_send.at[use], agx_recv.at[use, x],
                    device(y, along_x(f), z, h),
                ).start()
    def gathered(slots, use, source):
        got(slots.at[source], agx_recv.at[use, source])

    def spans():
        for c in range(2):
            for i in range(tiles):
                first = (c * tiles + i) * planes
                yield c, slice(i * width, (i + 1) * width), slice(first, first + planes)

    def unpack(pad, blocks, at_x):
        for c, at, own in spans():
            pad[c, pl.ds(at_x * gz, gz), 0:planes, at] = blocks[at_x, :, own, :]

    span = gz * PAD

    def rows_of(ref, targets):
        return jnp.concatenate(
            [ref[pl.ds(pl.multiple_of(to * span, span), span), :] for to in targets], axis=0
        )

    def padded_of(ref, c, targets):
        return jnp.concatenate(
            [ref[c, pl.ds(to * gz, gz)].reshape(span, length) for to in targets], axis=0
        )

    lane_sign = jnp.where(
        lax.broadcasted_iota(jnp.int32, (1, pair), 1) < pair // 2, 1.0, -1.0
    ).astype(F32)

    def group(value, r):
        return value[:, r * pair : (r + 1) * pair]

    def with_turned(value, sign):
        turned = [
            pltpu.roll(group(value, r), pair // 2, 1) * (sign * lane_sign) for r in range(3)
        ]
        return split(jnp.concatenate([value, jnp.concatenate(turned, axis=1)], axis=0))

    def to_lines(spectrum, use):
        pieces = with_turned(spectrum, -1.0)
        if use == 0:
            table_copies[0].wait()
        u_send[use] = table_times(back, other, pieces)
        remote(
            u_send.at[use], u_pair.at[use, h], core_send.at[use], core_recv.at[use], sibling
        ).start()
        u_pair[use, h] = table_times(back, h, pieces)

    def to_image(use, targets):
        first, second = rows_of(u_pair.at[use, 0], targets), rows_of(u_pair.at[use, 1], targets)
        parts = []
        for r in range(3):
            wide = jnp.concatenate([group(first, r), group(second, r)], axis=1)
            product = times_table(split(wide), home, r)
            parts.append((product[:, 0:third], product[:, third : 2 * third]))
        parts = thirds(parts, -1.0)
        return [jnp.concatenate([part[c] for part in parts], axis=1) for c in range(2)]

    def coil_sum(use, image_rows, hooks):
        order = nearest(gz)[::-1]
        for half in ((gx // 2, 1), (gx - 1, 0)):
            targets = [along_x(f) for f in half]
            re, im = image_rows(targets)
            s_re, s_im = padded_of(s_pad, 0, targets), padded_of(s_pad, 1, targets)
            sums = (s_re * re + s_im * im, s_re * im - s_im * re)
            for k, to in enumerate(targets):
                for c, at, own in spans():
                    block = sums[c][k * span : (k + 1) * span].reshape(gz, PAD, length)
                    part[use, to, :, own, :] = block[:, 0:planes, at]
                if half[k] == 0:
                    continue
                for i, d in enumerate(order):
                    remote(
                        part.at[use, to, along_z(d)], rx.at[use, x, i],
                        rsx_send.at[use], rsx_recv.at[use, x, i], device(y, to, z, h),
                    ).start()
        hooks[0]()
        for i, d in enumerate(order):
            target = along_z(d)
            total = part[use, x, target]
            for f in nearest(gx)[1:]:
                source = along_x(f)
                got(rx.at[use, source, i], rsx_recv.at[use, source, i])
                total = total + rx[use, source, i]
            q[use, i] = total
            if d != 0:
                remote(
                    q.at[use, i], rz.at[use, z], rsz_send.at[use], rsz_recv.at[use, z],
                    device(y, x, target, h),
                ).start()
        hooks[1]()
        block = q[use, gz - 1]
        for d in nearest(gz)[1:]:
            source = along_z(d)
            got(rz.at[use, source], rsz_recv.at[use, source])
            block = block + rz[use, source]
        return block

    def start_gather(block, it):
        ag[it, x, z] = block
        mine = ag.at[it, x, z]
        for d in nearest(gz)[1:]:
            remote(
                mine, mine, agz_send.at[it], agz_recv.at[it, z], device(y, x, along_z(d), h)
            ).start()
        for k, (c, at, own) in enumerate(spans()):
            hz_send[it, 0, k : k + 1, :] = ag[it, x, z, own.start : own.start + 1, :]
            hz_send[it, 1, k : k + 1, :] = ag[it, x, z, own.stop - 1 : own.stop, :]
        for i, target in enumerate(((y, below), (y, above))):
            remote(
                hz_send.at[it, i], hz_recv.at[it, i], halo_send.at[it, i], halo_recv.at[it, i],
                target,
            ).start()
        for i, d in enumerate((gy - 1, 1)):
            remote(
                mine, hx_recv.at[it, i], halo_send.at[it, 2 + i], halo_recv.at[it, 2 + i],
                device(along_y(d), x, z, h),
            ).start()

    row_ids = lax.broadcasted_iota(jnp.int32, (PAD, length), 0)
    lane_ids = lax.broadcasted_iota(jnp.int32, (PAD, length), 1)

    def variation(it):
        for i in range(2):
            got(hz_recv.at[it, i], halo_recv.at[it, i])
            got(hx_recv.at[it, i], halo_recv.at[it, 2 + i])
        first = (slab > 0).astype(F32)
        last = (slab < slabs - 1).astype(F32)
        x_first = (y > 0).astype(F32)
        x_last = (y < gy - 1).astype(F32)
        for k, (c, at, own) in enumerate(spans()):
            frame[c, 1 : planes + 1, at] = ag[it, x, z, own, :]
            frame[c, planes + 1 : planes + 2, at] = hz_recv[it, 0, k : k + 1, :] * last
            frame[c, 0:1, at] = hz_recv[it, 1, k : k + 1, :] * first
            xframe[0, c, 1 : planes + 1, at] = hx_recv[it, 0, own, :] * x_last
            xframe[1, c, 1 : planes + 1, at] = hx_recv[it, 1, own, :] * x_first
        for c in range(2):
            v = frame[c]
            flux = wframe[0] * (pltpu.roll(v, PAD - 1, 0) - v)
            out = pltpu.roll(flux, 1, 0) - flux
            out = out + wframe[2] * (v - xframe[1, c]) - wframe[1] * (xframe[0, c] - v)
            ahead = jnp.where(lane_ids < length - 1, pltpu.roll(v, length - 1, 1), 0.0)
            flux = wframe[3] * (ahead - v)
            out = out + jnp.where(lane_ids > 0, pltpu.roll(flux, 1, 1), 0.0) - flux
            frame[c] = out
        for c, at, own in spans():
            smooth[it, own, :] = frame[c, 1 : planes + 1, at]

    def lanes(value):
        return jnp.sum(value, axis=0, keepdims=True)

    tile_rows = lax.broadcasted_iota(jnp.int32, ar_y.shape[2:], 0)

    def start_sums(values, it):
        tile = jnp.zeros(ar_y.shape[2:], F32)
        for i, value in enumerate(values):
            tile = jnp.where(tile_rows == i, value, tile)
        ar_y[it, y] = tile
        for d in range(1, gy):
            remote(
                ar_y.at[it, y], ar_y.at[it, y], ary_send.at[it], ary_recv.at[it, y],
                device(along_y(d), x, z, h),
            ).start()

    def total_of(slots, it, count):
        total = slots[it, 0]
        for i in range(1, count):
            total = total + slots[it, i]
        return total

    def sums_z(it):
        for d in range(1, gy):
            got(ar_y.at[it, along_y(d)], ary_recv.at[it, along_y(d)])
        ar_z[it, z] = total_of(ar_y, it, gy)
        for d in range(1, gz):
            remote(
                ar_z.at[it, z], ar_z.at[it, z], arz_send.at[it], arz_recv.at[it, z],
                device(y, x, along_z(d), h),
            ).start()

    def sums_x(it):
        for d in range(1, gz):
            got(ar_z.at[it, along_z(d)], arz_recv.at[it, along_z(d)])
        mine = x * 2 + h
        ar_x[it, mine] = total_of(ar_z, it, gz)
        for d in range(1, 2 * gx):
            to = (mine + d) % (2 * gx)
            remote(
                ar_x.at[it, mine], ar_x.at[it, mine], arx_send.at[it], arx_recv.at[it, mine],
                device(y, to // 2, z, to % 2),
            ).start()

    def finish_sums(it, count):
        mine = x * 2 + h
        for d in range(1, 2 * gx):
            source = (mine + d) % (2 * gx)
            got(ar_x.at[it, source], arx_recv.at[it, source])
        total = total_of(ar_x, it, 2 * gx)
        return [jnp.sum(jnp.where(tile_rows == i, total, 0.0)) for i in range(count)]

    def operator(block, it, sums):
        gather(ag.at[it], it)
        variation(it)
        if it == 0:
            table_copies[2].wait()
        for half in ((0, 1), (gx - 1, gx // 2)):
            targets = [along_x(f) for f in half]
            for f, source in zip(half, targets):
                if f != 0:
                    gathered(ag.at[it], it, source)
                unpack(v_pad, ag.at[it], source)
            v_re, v_im = padded_of(v_pad, 0, targets), padded_of(v_pad, 1, targets)
            s_re, s_im = padded_of(s_pad, 0, targets), padded_of(s_pad, 1, targets)
            coil_re, coil_im = s_re * v_re - s_im * v_im, s_re * v_im + s_im * v_re
            cuts = [slice(a * third, (a + 1) * third) for a in range(3)]
            parts = thirds([(coil_re[:, at], coil_im[:, at]) for at in cuts], 1.0)
            for r in range(3):
                product = times_table(split(jnp.concatenate(parts[r], axis=1)), right, r)
                for core in range(2):
                    value = group(product, core)
                    for k, source in enumerate(targets):
                        here = pl.ds(pl.multiple_of(source * span, span), span)
                        t_pair[it, core, here, r * pair : (r + 1) * pair] = value[
                            k * span : (k + 1) * span
                        ]
            for f, source in zip(half, targets):
                here = pl.ds(pl.multiple_of(source * span, span), span)
                remote(
                    t_pair.at[it, other, here, :], t_recv.at[it, here, :],
                    swap_send.at[it, f], swap_recv.at[it, f], sibling,
                ).start()
        if it == 0:
            table_copies[3].wait()
        spectrum = table_times(left, h, with_turned(t_pair[it, h], 1.0))
        for f in range(gx):
            here = pl.ds(pl.multiple_of(along_x(f) * span, span), span)
            got(t_recv.at[it, here, :], swap_recv.at[it, f])
        spectrum = spectrum + table_times(left, other, with_turned(t_recv[it], 1.0))
        spectrum = spectrum * mask_t[...]
        power = jnp.sum(spectrum * spectrum, axis=0, keepdims=True)
        folded = power[:, 0:width]
        for i in range(1, power.shape[1] // width):
            folded = folded + power[:, i * width : (i + 1) * width]
        start_sums([folded + lanes(block * smooth[it])] + sums, it)
        to_lines(spectrum, 1 + it)
        got(u_pair.at[1 + it, other], core_recv.at[1 + it])
        return coil_sum(
            1 + it, partial(to_image, 1 + it), (lambda: sums_z(it), lambda: sums_x(it))
        ) + smooth[it]

    got(wz_recv, w_recv.at[0])
    got(wx_recv, w_recv.at[1])
    wframe[0, 1 : planes + 1, :] = w_ref[0, :, 0, :]
    wframe[0, 0:1, :] = wz_recv[0:1, :] * (slab > 0).astype(F32)
    wframe[1, 1 : planes + 1, :] = w_ref[1, :, 0, :]
    wframe[2, 1 : planes + 1, :] = wx_recv[:, 0, :] * (y > 0).astype(F32)
    wframe[3, 1 : planes + 1, :] = w_ref[2, :, 0, :]

    for t in range(steps):
        over_z(t)
        if t + 2 < steps:
            sent(wy.at[t, pl.ds(0, gy - 1)], y_send.at[t])
            over_y(t + 2)
        if t > 0:
            over_x(t - 1)
        if t == 1:
            gather(mb, 2)

    def unpack_lines(blocks, both):
        for c, at, own in spans():
            for j in range(planes):
                row = (j % 3) * pair + c * (pair // 2) + (j // 3) * chips
                k = own.start + j - (c * tiles * planes if both else 0)
                k_pad[row : row + chips, at] = blocks[:, :, k, :].reshape(chips, width)
        return k_pad[...].T

    for f in range(1, gx):
        gathered(mb, 2, along_x(f))
    mask_t[...] = unpack_lines(mb, True)
    arrived(0)
    to_lines(unpack_lines(kx, False), 0)
    over_x(steps - 1)
    table_copies[1].wait()
    got(u_pair.at[0, other], core_recv.at[0])
    for c, value in enumerate(to_image(0, list(range(gx)))):
        early[c] = value
    arrived(1)
    for f in range(gx):
        unpack(s_pad, sx, along_x(f))
    first = coil_sum(
        0,
        lambda targets: [rows_of(early.at[c], targets) for c in range(2)],
        (lambda: None, lambda: None),
    )

    start_gather(first, 0)
    applied = operator(first, 0, [lanes(first * first)])
    curvature, norm = finish_sums(0, 2)
    step = norm / curvature
    second = first - step * applied
    start_gather(second, 1)
    hold[0] = applied
    hold[1] = second
    fresh = operator(second, 1, [lanes(second * second), lanes(second * applied)])
    applied, second = hold[0], hold[1]
    first = ag[0, x, z]
    own, norm_next, cross = finish_sums(1, 3)
    ratio = norm_next / norm
    curvature_next = own + 2.0 * ratio * cross + ratio * ratio * curvature
    step_next = norm_next / curvature_next
    hold[0] = step * first + step_next * (second + ratio * first)
    hold[1] = second - step_next * (fresh + ratio * applied)
    for c, at, own in spans():
        x_out[c, :, at] = hold[0, own, :]
        r_out[c, :, at] = hold[1, own, :]

    for t in range(steps):
        if t + 2 >= steps:
            sent(wy.at[t, pl.ds(0, gy - 1)], y_send.at[t])
        sent(wz.at[t, pl.ds(0, gz - 1)], z_send.at[t])
        if (t + 1) % gx != 0:
            sent(wz.at[t], x_send.at[t])
    for i in range(2):
        sent(ag.at[i, 0, pl.ds(0, gz - 1)], agz_send.at[i])
        sent(ag.at[i, pl.ds(0, gx - 1)], agx_send.at[i])
        sent(ar_y.at[i, pl.ds(0, gy - 1)], ary_send.at[i])
        sent(ar_z.at[i, pl.ds(0, gz - 1)], arz_send.at[i])
        sent(ar_x.at[i, pl.ds(0, 2 * gx - 1)], arx_send.at[i])
        for f in range(gx):
            sent(t_recv.at[i, 0:span, :], swap_send.at[i, f])
        for j in range(2):
            sent(hz_send.at[i, j], halo_send.at[i, j])
            sent(hx_recv.at[i, j], halo_send.at[i, 2 + j])
    for use in range(3):
        sent(rx.at[use, pl.ds(0, gx - 1)], rsx_send.at[use])
        sent(rz.at[use, pl.ds(0, gz - 1)], rsz_send.at[use])
        sent(u_send.at[use], core_send.at[use])
    sent(mb.at[0, pl.ds(0, gz - 1)], agz_send.at[2])
    sent(mb.at[pl.ds(0, gx - 1)], agx_send.at[2])
    sent(wz_send, w_send.at[0])
    sent(wx_recv, w_send.at[1])


def body(sizes, kspace, coil_maps, sampling, variation_weights):
    gx, gy, gz, planes, length, lanes = sizes
    chips = gx * gz
    rows = chips * PAD
    tiles = length // lanes
    tables = fourier_tables(length, chips, planes)
    block = (2 * tiles * planes, lanes)
    rounds = (2 * gx, gy) + block
    last = (gx, gz) + block
    dma = pltpu.SemaphoreType.DMA
    vmem = pltpu.VMEM
    scratch = [vmem(table.shape, BF16) for table in tables]
    wires = (gy, gx) + block
    scratch += [
        vmem((2, gx, planes, gy, length), F32),
        vmem((2, gx, tiles, planes * gy, lanes), F32),
        vmem(wires, F32),
        vmem(wires, F32),
    ]
    scratch += [vmem(shape, F32) for shape in (rounds, rounds, last, last)]
    scratch += [
        vmem((gx, gz, tiles * planes, lanes), F32),
        vmem((length, length), F32),
        vmem((2, chips, PAD, length), F32),
        vmem((2, chips, PAD, length), F32),
        vmem((length, length), F32),
        vmem((2, 2, rows, length), F32),
        vmem((2, rows, length), F32),
        vmem((3, rows, length), F32),
        vmem((3, 2, rows, length), F32),
        vmem((3,) + last, F32),
        vmem((3,) + last, F32),
        vmem((3, gz) + block, F32),
        vmem((3, gz) + block, F32),
        vmem((2,) + last, F32),
        vmem((PAD, length), F32),
        vmem((PAD, length), F32),
        vmem((planes, 1, length), F32),
        vmem((2, 2, 2 * tiles, lanes), F32),
        vmem((2, 2, 2 * tiles, lanes), F32),
        vmem((2, 2) + block, F32),
        vmem((2, PAD, length), F32),
        vmem((2, 2, PAD, length), F32),
        vmem((4, PAD, length), F32),
        vmem((2,) + block, F32),
        vmem((2,) + block, F32),
        vmem((2, rows, length), F32),
        vmem((2, gy, 8, lanes), F32),
        vmem((2, gz, 8, lanes), F32),
        vmem((2, 2 * gx, 8, lanes), F32),
        dma((4,)), dma(()),
        dma((2 * gx,)), dma((2 * gx,)), dma((2 * gx,)), dma((2 * gx,)), dma((2 * gx,)),
        dma((2 * gx,)),
        dma((3,)), dma((3, gz)), dma((3,)), dma((3, gx)),
        dma((3,)), dma((3, gx, gz)), dma((3,)), dma((3, gz)),
        dma((3,)), dma((3,)), dma((2, gx)), dma((2, gx)),
        dma((2,)), dma((2,)), dma((2, 4)), dma((2, 4)),
        dma((2,)), dma((2, gy)), dma((2,)), dma((2, gz)), dma((2,)), dma((2, 2 * gx)),
    ]
    in_vmem = pl.BlockSpec(memory_space=pltpu.VMEM)
    anywhere = pl.BlockSpec(memory_space=pl.ANY)
    image, residual = pl.pallas_call(
        partial(kernel, sizes),
        out_shape=[jax.ShapeDtypeStruct((2, planes, length), F32)] * 2,
        in_specs=[anywhere] + [in_vmem] * 3 + [anywhere] * 4,
        out_specs=[in_vmem] * 2,
        scratch_shapes=scratch,
        compiler_params=pltpu.CompilerParams(
            collective_id=0, has_side_effects=True, vmem_limit_bytes=58 * 2**20
        ),
    )(kspace, coil_maps, sampling, variation_weights, *[jnp.asarray(t) for t in tables])
    return image[:, :, None, :], residual[:, :, None, :]


def solution(mesh, gx=4, gz=8):
    gy = mesh.shape["coil"]

    def whole(kspace, coil_maps, sampling, variation_weights):
        length = kspace.shape[4]
        planes = length // (gx * gz * 2)
        sizes = (gx, gy, gz, planes, length, math.gcd(128, length, gx * gz * PAD))
        return jax.shard_map(
            partial(body, sizes),
            mesh=mesh,
            in_specs=(
                P(None, "coil", "slab", None, None),
                P(None, "coil", "slab", None, None),
                P("slab", None),
                P(None, "slab", "coil", None),
            ),
            out_specs=(P(None, "slab", "coil", None), P(None, "slab", "coil", None)),
            check_vma=False,
        )(kspace, coil_maps, sampling, variation_weights)

    return whole
```

```python
from functools import partial
import math

import jax
import jax.numpy as jnp
import numpy as np
from jax import lax
from jax.experimental import pallas as pl
from jax.experimental.pallas import tpu as pltpu
from jax.sharding import PartitionSpec as P

F32 = jnp.float32
BF16 = jnp.bfloat16
PAD = 8


def halves(table):
    high = table.astype(BF16)
    low = (table - high.astype(np.float32)).astype(BF16)
    return np.stack([high, low])


def fourier_tables(length, chips, planes):
    third = length // 3
    core, chip, plane = np.meshgrid(np.arange(2), np.arange(chips), np.arange(PAD), indexing="ij")
    owned = ((chip * 2 + core) * planes + plane).reshape(2, 1, -1)
    valid = (plane < planes).astype(np.float64).reshape(2, 1, -1) / math.sqrt(length)
    natural = np.arange(length, dtype=np.int64)
    angles = natural[None, :, None] * owned % length * (2.0 * math.pi / length)
    cosine, sine = np.cos(angles) * valid, np.sin(angles) * valid
    left = np.concatenate([cosine, sine], axis=2)
    back = np.concatenate([np.swapaxes(cosine, 1, 2), np.swapaxes(sine, 1, 2)], axis=2)
    right = []
    for r in range(3):
        columns = []
        for core in range(2):
            step, chip = np.meshgrid(np.arange(planes // 3), np.arange(chips), indexing="ij")
            lines = ((chip * 2 + core) * planes + 3 * step + r).reshape(1, -1)
            angles = np.arange(third)[:, None] * lines % length * (2.0 * math.pi / length)
            cosine, sine = np.cos(angles) / math.sqrt(length), np.sin(angles) / math.sqrt(length)
            columns.append(np.concatenate([cosine, sine], axis=0))
            columns.append(np.concatenate([-sine, cosine], axis=0))
        right.append(np.concatenate(columns, axis=1))
    right = np.stack(right)
    home = np.swapaxes(right, 1, 2)
    return tuple(halves(table.astype(np.float32)) for table in (right, left, back, home))


def thirds(parts, orient):
    (re0, im0), (re1, im1), (re2, im2) = parts
    turn = orient * math.sqrt(0.75)
    sum_re, sum_im = re1 + re2, im1 + im2
    dif_re, dif_im = turn * (re1 - re2), turn * (im1 - im2)
    mid_re, mid_im = re0 - 0.5 * sum_re, im0 - 0.5 * sum_im
    return (
        (re0 + sum_re, im0 + sum_im),
        (mid_re + dif_im, mid_im - dif_re),
        (mid_re - dif_im, mid_im + dif_re),
    )


def split(value):
    high = value.astype(BF16)
    return high, (value - high.astype(F32)).astype(BF16)


def dot(a, b):
    return jnp.dot(a, b, preferred_element_type=F32)


def times_table(value, table, which):
    high, low = value
    return (
        dot(high, table[0, which]) + dot(low, table[0, which]) + dot(high, table[1, which])
    )


def table_times(table, which, value):
    high, low = value
    return (
        dot(table[0, which], high) + dot(table[0, which], low) + dot(table[1, which], high)
    )


def nearest(count):
    offsets = [0]
    for d in range(1, count // 2):
        offsets += [d, -d]
    return offsets + [count // 2]


def kernel(
    sizes,
    k_hbm, s_raw, m_ref, w_ref, right_hbm, left_hbm, back_hbm, home_hbm,
    x_out, r_out,
    right, left, back, home,
    k_raw, stage, k_ref, s_ref,
    wy, wz, kx, sx, mb,
    mask_t, s_pad, v_pad, k_pad,
    t_pair, t_recv, u_send, u_pair,
    part, rx, q, rz, ag,
    wz_send, wz_recv, wx_recv, hz_send, hz_recv, hx_recv,
    frame, xframe, wframe, smooth, hold, early,
    ar_y, ar_z, ar_x,
    table_sem, k_sem,
    y_send, y_recv, z_send, z_recv, x_send, x_recv,
    agz_send, agz_recv, agx_send, agx_recv,
    rsx_send, rsx_recv, rsz_send, rsz_recv,
    core_send, core_recv, swap_send, swap_recv,
    w_send, w_recv, halo_send, halo_recv,
    ary_send, ary_recv, arz_send, arz_recv, arx_send, arx_recv,
):
    gx, gy, gz, planes, length, width = sizes
    chips = gx * gz
    rows = chips * PAD
    tiles = length // width
    third = length // 3
    pair = 2 * (planes // 3) * chips
    y = lax.axis_index("coil")
    slab = lax.axis_index("slab")
    x = slab // (gz * 2)
    z = (slab // 2) % gz
    h = slab % 2
    other = 1 - h

    def device(y_, x_, z_, h_):
        return (y_, (x_ * gz + z_) * 2 + h_)

    def remote(src, dst, send_sem, recv_sem, target):
        return pltpu.make_async_remote_copy(
            src_ref=src, dst_ref=dst, send_sem=send_sem, recv_sem=recv_sem,
            device_id=target, device_id_type=pl.DeviceIdType.MESH,
        )

    sibling = device(y, x, z, other)

    def got(dst, recv_sem):
        remote(dst, dst, recv_sem, recv_sem, sibling).wait_recv()

    def sent(src, send_sem):
        remote(src, src, send_sem, send_sem, sibling).wait_send()

    def along_y(d):
        return (y + d + gy) % gy

    def along_z(d):
        return (z + d + gz) % gz

    def along_x(d):
        return (x + d + gx) % gx

    k_copy = pltpu.make_async_copy(k_hbm, k_raw, k_sem)
    k_copy.start()
    table_copies = [
        pltpu.make_async_copy(src, dst, table_sem.at[i])
        for i, (src, dst) in enumerate(
            ((back_hbm, back), (home_hbm, home), (right_hbm, right), (left_hbm, left))
        )
    ]
    for copy in table_copies:
        copy.start()

    slabs = gx * gz * 2
    below = (slab + slabs - 1) % slabs
    above = (slab + 1) % slabs
    barrier = pltpu.get_barrier_semaphore()

    def greet(target):
        pl.semaphore_signal(barrier, inc=1, device_id=target, device_id_type=pl.DeviceIdType.MESH)

    for d in range(1, gy):
        greet(device(along_y(d), x, z, h))
    for d in range(1, gz):
        greet(device(y, x, along_z(d), h))
    for d in range(1, gx):
        greet(device(y, along_x(d), z, h))
        greet(device(y, along_x(d), z, other))
    greet(sibling)
    greet((y, jnp.where(h == 0, below, above)))
    for ref in (s_pad, v_pad, frame, xframe, wframe):
        ref[...] = jnp.zeros_like(ref)
    lines = m_ref[...].astype(F32)
    for i in range(tiles):
        mb[x, z, i * planes : (i + 1) * planes, :] = lines[:, i * width : (i + 1) * width]
    wz_send[0:1, :] = w_ref[0, planes - 1, :, :]

    def by_position(value_of, wires):
        for coil in range(gx):
            for c in range(2):
                value = value_of(c, coil).reshape(planes * gy, length)
                for i in range(tiles):
                    first = (c * tiles + i) * planes
                    stage[c, coil, i] = value[:, i * width : (i + 1) * width]
                    for to in range(gy):
                        wires[to, coil, first : first + planes, :] = stage[
                            c, coil, i, pl.ds(to, planes, stride=gy), :
                        ]

    k_copy.wait()
    by_position(lambda c, coil: k_raw[c, coil] * lines[:, None, :], k_ref)
    pl.semaphore_wait(barrier, (gy - 1) + (gz - 1) + 2 * (gx - 1) + 2)

    steps = 2 * gx
    sources = (k_ref, s_ref)
    ends = (kx, sx)

    def over_y(t):
        source, coil = sources[t // gx], along_x((t + 1) % gx)
        for d in nearest(gy)[:0:-1]:
            to = along_y(d)
            remote(
                source.at[to, coil], wy.at[t, y], y_send.at[t], y_recv.at[t], device(to, x, z, h)
            ).start()
        wy[t, y] = source[y, coil]

    def over_z(t):
        got(wy.at[t, pl.ds(0, gy - 1)], y_recv.at[t])
        for d in nearest(gz)[:0:-1]:
            to = along_z(d)
            remote(
                wy.at[t, to], wz.at[t, z], z_send.at[t], z_recv.at[t], device(y, x, to, h)
            ).start()
        wz[t, z] = wy[t, z]

    def over_x(t):
        got(wz.at[t, pl.ds(0, gz - 1)], z_recv.at[t])
        end = ends[t // gx]
        if (t + 1) % gx == 0:
            end[x] = wz[t]
        else:
            remote(
                wz.at[t], end.at[x], x_send.at[t], x_recv.at[t],
                device(y, along_x((t + 1) % gx), z, h),
            ).start()

    def arrived(i):
        for f in range(1, gx):
            got(ends[i].at[along_x(gx - f)], x_recv.at[i * gx + f - 1])

    over_y(0)
    over_y(1)
    by_position(lambda c, coil: s_raw[c, coil].astype(F32), s_ref)

    for d in nearest(gz)[1:]:
        remote(
            mb.at[x, z], mb.at[x, z], agz_send.at[2], agz_recv.at[2, z],
            device(y, x, along_z(d), h),
        ).start()
    remote(wz_send, wz_recv, w_send.at[0], w_recv.at[0], (y, above)).start()
    remote(w_ref.at[1], wx_recv, w_send.at[1], w_recv.at[1], device(along_y(1), x, z, h)).start()

    def gather(slots, use):
        for d in nearest(gz):
            block = slots.at[x, along_z(d)]
            if d != 0:
                got(block, agz_recv.at[use, along_z(d)])
            for f in nearest(gx)[:0:-1]:
                remote(
                    block, block, agx_send.at[use], agx_recv.at[use, x],
                    device(y, along_x(f), z, h),
                ).start()
    def gathered(slots, use, source):
        got(slots.at[source], agx_recv.at[use, source])

    def spans():
        for c in range(2):
            for i in range(tiles):
                first = (c * tiles + i) * planes
                yield c, slice(i * width, (i + 1) * width), slice(first, first + planes)

    def unpack(pad, blocks, at_x):
        for c, at, own in spans():
            pad[c, pl.ds(at_x * gz, gz), 0:planes, at] = blocks[at_x, :, own, :]

    span = gz * PAD

    def rows_of(ref, targets):
        return jnp.concatenate(
            [ref[pl.ds(pl.multiple_of(to * span, span), span), :] for to in targets], axis=0
        )

    def padded_of(ref, c, targets):
        return jnp.concatenate(
            [ref[c, pl.ds(to * gz, gz)].reshape(span, length) for to in targets], axis=0
        )

    lane_sign = jnp.where(
        lax.broadcasted_iota(jnp.int32, (1, pair), 1) < pair // 2, 1.0, -1.0
    ).astype(F32)

    def group(value, r):
        return value[:, r * pair : (r + 1) * pair]

    def with_turned(value, sign):
        turned = [
            pltpu.roll(group(value, r), pair // 2, 1) * (sign * lane_sign) for r in range(3)
        ]
        return split(jnp.concatenate([value, jnp.concatenate(turned, axis=1)], axis=0))

    def to_lines(spectrum, use):
        pieces = with_turned(spectrum, -1.0)
        if use == 0:
            table_copies[0].wait()
        u_send[use] = table_times(back, other, pieces)
        for f in (gx // 2, 1, gx - 1, 0):
            here = pl.ds(pl.multiple_of(along_x(f) * span, span), span)
            remote(
                u_send.at[use, here, :], u_pair.at[use, h, here, :],
                core_send.at[use, f], core_recv.at[use, f], sibling,
            ).start()
        u_pair[use, h] = table_times(back, h, pieces)

    def to_image(use, targets, half):
        for f in range(gx) if use == 0 else half:
            here = pl.ds(pl.multiple_of(along_x(f) * span, span), span)
            got(u_pair.at[use, other, here, :], core_recv.at[use, f])
        first, second = rows_of(u_pair.at[use, 0], targets), rows_of(u_pair.at[use, 1], targets)
        parts = []
        for r in range(3):
            wide = jnp.concatenate([group(first, r), group(second, r)], axis=1)
            product = times_table(split(wide), home, r)
            parts.append((product[:, 0:third], product[:, third : 2 * third]))
        parts = thirds(parts, -1.0)
        return [jnp.concatenate([part[c] for part in parts], axis=1) for c in range(2)]

    def coil_sum(use, image_rows, hooks):
        order = nearest(gz)[::-1]
        for half in ((gx // 2, 1), (gx - 1, 0)):
            targets = [along_x(f) for f in half]
            re, im = image_rows(targets, half)
            s_re, s_im = padded_of(s_pad, 0, targets), padded_of(s_pad, 1, targets)
            sums = (s_re * re + s_im * im, s_re * im - s_im * re)
            for k, to in enumerate(targets):
                for c, at, own in spans():
                    block = sums[c][k * span : (k + 1) * span].reshape(gz, PAD, length)
                    part[use, to, :, own, :] = block[:, 0:planes, at]
                if half[k] == 0:
                    continue
                for i, d in enumerate(order):
                    remote(
                        part.at[use, to, along_z(d)], rx.at[use, x, i],
                        rsx_send.at[use], rsx_recv.at[use, x, i], device(y, to, z, h),
                    ).start()
        hooks[0]()
        for i, d in enumerate(order):
            target = along_z(d)
            total = part[use, x, target]
            for f in nearest(gx)[1:]:
                source = along_x(f)
                got(rx.at[use, source, i], rsx_recv.at[use, source, i])
                total = total + rx[use, source, i]
            q[use, i] = total
            if d != 0:
                remote(
                    q.at[use, i], rz.at[use, z], rsz_send.at[use], rsz_recv.at[use, z],
                    device(y, x, target, h),
                ).start()
        hooks[1]()
        block = q[use, gz - 1]
        for d in nearest(gz)[1:]:
            source = along_z(d)
            got(rz.at[use, source], rsz_recv.at[use, source])
            block = block + rz[use, source]
        return block

    def start_gather(block, it):
        ag[it, x, z] = block
        mine = ag.at[it, x, z]
        for d in nearest(gz)[1:]:
            remote(
                mine, mine, agz_send.at[it], agz_recv.at[it, z], device(y, x, along_z(d), h)
            ).start()
        for k, (c, at, own) in enumerate(spans()):
            hz_send[it, 0, k : k + 1, :] = ag[it, x, z, own.start : own.start + 1, :]
            hz_send[it, 1, k : k + 1, :] = ag[it, x, z, own.stop - 1 : own.stop, :]
        for i, target in enumerate(((y, below), (y, above))):
            remote(
                hz_send.at[it, i], hz_recv.at[it, i], halo_send.at[it, i], halo_recv.at[it, i],
                target,
            ).start()
        for i, d in enumerate((gy - 1, 1)):
            remote(
                mine, hx_recv.at[it, i], halo_send.at[it, 2 + i], halo_recv.at[it, 2 + i],
                device(along_y(d), x, z, h),
            ).start()

    row_ids = lax.broadcasted_iota(jnp.int32, (PAD, length), 0)
    lane_ids = lax.broadcasted_iota(jnp.int32, (PAD, length), 1)

    def variation(it):
        for i in range(2):
            got(hz_recv.at[it, i], halo_recv.at[it, i])
            got(hx_recv.at[it, i], halo_recv.at[it, 2 + i])
        first = (slab > 0).astype(F32)
        last = (slab < slabs - 1).astype(F32)
        x_first = (y > 0).astype(F32)
        x_last = (y < gy - 1).astype(F32)
        for k, (c, at, own) in enumerate(spans()):
            frame[c, 1 : planes + 1, at] = ag[it, x, z, own, :]
            frame[c, planes + 1 : planes + 2, at] = hz_recv[it, 0, k : k + 1, :] * last
            frame[c, 0:1, at] = hz_recv[it, 1, k : k + 1, :] * first
            xframe[0, c, 1 : planes + 1, at] = hx_recv[it, 0, own, :] * x_last
            xframe[1, c, 1 : planes + 1, at] = hx_recv[it, 1, own, :] * x_first
        for c in range(2):
            v = frame[c]
            flux = wframe[0] * (pltpu.roll(v, PAD - 1, 0) - v)
            out = pltpu.roll(flux, 1, 0) - flux
            out = out + wframe[2] * (v - xframe[1, c]) - wframe[1] * (xframe[0, c] - v)
            ahead = jnp.where(lane_ids < length - 1, pltpu.roll(v, length - 1, 1), 0.0)
            flux = wframe[3] * (ahead - v)
            out = out + jnp.where(lane_ids > 0, pltpu.roll(flux, 1, 1), 0.0) - flux
            frame[c] = out
        for c, at, own in spans():
            smooth[it, own, :] = frame[c, 1 : planes + 1, at]

    def lanes(value):
        return jnp.sum(value, axis=0, keepdims=True)

    tile_rows = lax.broadcasted_iota(jnp.int32, ar_y.shape[2:], 0)

    def start_sums(values, it):
        tile = jnp.zeros(ar_y.shape[2:], F32)
        for i, value in enumerate(values):
            tile = jnp.where(tile_rows == i, value, tile)
        ar_y[it, y] = tile
        for d in range(1, gy):
            remote(
                ar_y.at[it, y], ar_y.at[it, y], ary_send.at[it], ary_recv.at[it, y],
                device(along_y(d), x, z, h),
            ).start()

    def total_of(slots, it, count):
        total = slots[it, 0]
        for i in range(1, count):
            total = total + slots[it, i]
        return total

    def sums_z(it):
        for d in range(1, gy):
            got(ar_y.at[it, along_y(d)], ary_recv.at[it, along_y(d)])
        ar_z[it, z] = total_of(ar_y, it, gy)
        for d in range(1, gz):
            remote(
                ar_z.at[it, z], ar_z.at[it, z], arz_send.at[it], arz_recv.at[it, z],
                device(y, x, along_z(d), h),
            ).start()

    def sums_x(it):
        for d in range(1, gz):
            got(ar_z.at[it, along_z(d)], arz_recv.at[it, along_z(d)])
        mine = x * 2 + h
        ar_x[it, mine] = total_of(ar_z, it, gz)
        for d in range(1, 2 * gx):
            to = (mine + d) % (2 * gx)
            remote(
                ar_x.at[it, mine], ar_x.at[it, mine], arx_send.at[it], arx_recv.at[it, mine],
                device(y, to // 2, z, to % 2),
            ).start()

    def finish_sums(it, count):
        mine = x * 2 + h
        for d in range(1, 2 * gx):
            source = (mine + d) % (2 * gx)
            got(ar_x.at[it, source], arx_recv.at[it, source])
        total = total_of(ar_x, it, 2 * gx)
        return [jnp.sum(jnp.where(tile_rows == i, total, 0.0)) for i in range(count)]

    def operator(block, it, sums):
        gather(ag.at[it], it)
        variation(it)
        if it == 0:
            table_copies[2].wait()
        for half in ((0, 1), (gx - 1, gx // 2)):
            targets = [along_x(f) for f in half]
            for f, source in zip(half, targets):
                if f != 0:
                    gathered(ag.at[it], it, source)
                unpack(v_pad, ag.at[it], source)
            v_re, v_im = padded_of(v_pad, 0, targets), padded_of(v_pad, 1, targets)
            s_re, s_im = padded_of(s_pad, 0, targets), padded_of(s_pad, 1, targets)
            coil_re, coil_im = s_re * v_re - s_im * v_im, s_re * v_im + s_im * v_re
            cuts = [slice(a * third, (a + 1) * third) for a in range(3)]
            parts = thirds([(coil_re[:, at], coil_im[:, at]) for at in cuts], 1.0)
            for r in range(3):
                product = times_table(split(jnp.concatenate(parts[r], axis=1)), right, r)
                for core in range(2):
                    value = group(product, core)
                    for k, source in enumerate(targets):
                        here = pl.ds(pl.multiple_of(source * span, span), span)
                        t_pair[it, core, here, r * pair : (r + 1) * pair] = value[
                            k * span : (k + 1) * span
                        ]
            for f, source in zip(half, targets):
                here = pl.ds(pl.multiple_of(source * span, span), span)
                remote(
                    t_pair.at[it, other, here, :], t_recv.at[it, here, :],
                    swap_send.at[it, f], swap_recv.at[it, f], sibling,
                ).start()
        if it == 0:
            table_copies[3].wait()
        spectrum = table_times(left, h, with_turned(t_pair[it, h], 1.0))
        for f in range(gx):
            here = pl.ds(pl.multiple_of(along_x(f) * span, span), span)
            got(t_recv.at[it, here, :], swap_recv.at[it, f])
        spectrum = spectrum + table_times(left, other, with_turned(t_recv[it], 1.0))
        spectrum = spectrum * mask_t[...]
        power = jnp.sum(spectrum * spectrum, axis=0, keepdims=True)
        folded = power[:, 0:width]
        for i in range(1, power.shape[1] // width):
            folded = folded + power[:, i * width : (i + 1) * width]
        start_sums([folded + lanes(block * smooth[it])] + sums, it)
        to_lines(spectrum, 1 + it)
        return coil_sum(
            1 + it, partial(to_image, 1 + it), (lambda: sums_z(it), lambda: sums_x(it))
        ) + smooth[it]

    got(wz_recv, w_recv.at[0])
    got(wx_recv, w_recv.at[1])
    wframe[0, 1 : planes + 1, :] = w_ref[0, :, 0, :]
    wframe[0, 0:1, :] = wz_recv[0:1, :] * (slab > 0).astype(F32)
    wframe[1, 1 : planes + 1, :] = w_ref[1, :, 0, :]
    wframe[2, 1 : planes + 1, :] = wx_recv[:, 0, :] * (y > 0).astype(F32)
    wframe[3, 1 : planes + 1, :] = w_ref[2, :, 0, :]

    for t in range(steps):
        over_z(t)
        if t + 2 < steps:
            sent(wy.at[t, pl.ds(0, gy - 1)], y_send.at[t])
            over_y(t + 2)
        if t > 0:
            over_x(t - 1)
        if t == 1:
            gather(mb, 2)

    def unpack_lines(blocks, both):
        for c, at, own in spans():
            for j in range(planes):
                row = (j % 3) * pair + c * (pair // 2) + (j // 3) * chips
                k = own.start + j - (c * tiles * planes if both else 0)
                k_pad[row : row + chips, at] = blocks[:, :, k, :].reshape(chips, width)
        return k_pad[...].T

    for f in range(1, gx):
        gathered(mb, 2, along_x(f))
    mask_t[...] = unpack_lines(mb, True)
    arrived(0)
    to_lines(unpack_lines(kx, False), 0)
    over_x(steps - 1)
    table_copies[1].wait()
    for c, value in enumerate(to_image(0, list(range(gx)), None)):
        early[c] = value
    arrived(1)
    for f in range(gx):
        unpack(s_pad, sx, along_x(f))
    first = coil_sum(
        0,
        lambda targets, half: [rows_of(early.at[c], targets) for c in range(2)],
        (lambda: None, lambda: None),
    )

    start_gather(first, 0)
    applied = operator(first, 0, [lanes(first * first)])
    curvature, norm = finish_sums(0, 2)
    step = norm / curvature
    second = first - step * applied
    start_gather(second, 1)
    hold[0] = applied
    hold[1] = second
    fresh = operator(second, 1, [lanes(second * second), lanes(second * applied)])
    applied, second = hold[0], hold[1]
    first = ag[0, x, z]
    own, norm_next, cross = finish_sums(1, 3)
    ratio = norm_next / norm
    curvature_next = own + 2.0 * ratio * cross + ratio * ratio * curvature
    step_next = norm_next / curvature_next
    hold[0] = step * first + step_next * (second + ratio * first)
    hold[1] = second - step_next * (fresh + ratio * applied)
    for c, at, own in spans():
        x_out[c, :, at] = hold[0, own, :]
        r_out[c, :, at] = hold[1, own, :]

    for t in range(steps):
        if t + 2 >= steps:
            sent(wy.at[t, pl.ds(0, gy - 1)], y_send.at[t])
        sent(wz.at[t, pl.ds(0, gz - 1)], z_send.at[t])
        if (t + 1) % gx != 0:
            sent(wz.at[t], x_send.at[t])
    for i in range(2):
        sent(ag.at[i, 0, pl.ds(0, gz - 1)], agz_send.at[i])
        sent(ag.at[i, pl.ds(0, gx - 1)], agx_send.at[i])
        sent(ar_y.at[i, pl.ds(0, gy - 1)], ary_send.at[i])
        sent(ar_z.at[i, pl.ds(0, gz - 1)], arz_send.at[i])
        sent(ar_x.at[i, pl.ds(0, 2 * gx - 1)], arx_send.at[i])
        for f in range(gx):
            sent(t_recv.at[i, 0:span, :], swap_send.at[i, f])
        for j in range(2):
            sent(hz_send.at[i, j], halo_send.at[i, j])
            sent(hx_recv.at[i, j], halo_send.at[i, 2 + j])
    for use in range(3):
        sent(rx.at[use, pl.ds(0, gx - 1)], rsx_send.at[use])
        sent(rz.at[use, pl.ds(0, gz - 1)], rsz_send.at[use])
        for f in range(gx):
            sent(u_send.at[use, 0:span, :], core_send.at[use, f])
    sent(mb.at[0, pl.ds(0, gz - 1)], agz_send.at[2])
    sent(mb.at[pl.ds(0, gx - 1)], agx_send.at[2])
    sent(wz_send, w_send.at[0])
    sent(wx_recv, w_send.at[1])


def body(sizes, kspace, coil_maps, sampling, variation_weights):
    gx, gy, gz, planes, length, lanes = sizes
    chips = gx * gz
    rows = chips * PAD
    tiles = length // lanes
    tables = fourier_tables(length, chips, planes)
    block = (2 * tiles * planes, lanes)
    rounds = (2 * gx, gy) + block
    last = (gx, gz) + block
    dma = pltpu.SemaphoreType.DMA
    vmem = pltpu.VMEM
    scratch = [vmem(table.shape, BF16) for table in tables]
    wires = (gy, gx) + block
    scratch += [
        vmem((2, gx, planes, gy, length), F32),
        vmem((2, gx, tiles, planes * gy, lanes), F32),
        vmem(wires, F32),
        vmem(wires, F32),
    ]
    scratch += [vmem(shape, F32) for shape in (rounds, rounds, last, last)]
    scratch += [
        vmem((gx, gz, tiles * planes, lanes), F32),
        vmem((length, length), F32),
        vmem((2, chips, PAD, length), F32),
        vmem((2, chips, PAD, length), F32),
        vmem((length, length), F32),
        vmem((2, 2, rows, length), F32),
        vmem((2, rows, length), F32),
        vmem((3, rows, length), F32),
        vmem((3, 2, rows, length), F32),
        vmem((3,) + last, F32),
        vmem((3,) + last, F32),
        vmem((3, gz) + block, F32),
        vmem((3, gz) + block, F32),
        vmem((2,) + last, F32),
        vmem((PAD, length), F32),
        vmem((PAD, length), F32),
        vmem((planes, 1, length), F32),
        vmem((2, 2, 2 * tiles, lanes), F32),
        vmem((2, 2, 2 * tiles, lanes), F32),
        vmem((2, 2) + block, F32),
        vmem((2, PAD, length), F32),
        vmem((2, 2, PAD, length), F32),
        vmem((4, PAD, length), F32),
        vmem((2,) + block, F32),
        vmem((2,) + block, F32),
        vmem((2, rows, length), F32),
        vmem((2, gy, 8, lanes), F32),
        vmem((2, gz, 8, lanes), F32),
        vmem((2, 2 * gx, 8, lanes), F32),
        dma((4,)), dma(()),
        dma((2 * gx,)), dma((2 * gx,)), dma((2 * gx,)), dma((2 * gx,)), dma((2 * gx,)),
        dma((2 * gx,)),
        dma((3,)), dma((3, gz)), dma((3,)), dma((3, gx)),
        dma((3,)), dma((3, gx, gz)), dma((3,)), dma((3, gz)),
        dma((3, gx)), dma((3, gx)), dma((2, gx)), dma((2, gx)),
        dma((2,)), dma((2,)), dma((2, 4)), dma((2, 4)),
        dma((2,)), dma((2, gy)), dma((2,)), dma((2, gz)), dma((2,)), dma((2, 2 * gx)),
    ]
    in_vmem = pl.BlockSpec(memory_space=pltpu.VMEM)
    anywhere = pl.BlockSpec(memory_space=pl.ANY)
    image, residual = pl.pallas_call(
        partial(kernel, sizes),
        out_shape=[jax.ShapeDtypeStruct((2, planes, length), F32)] * 2,
        in_specs=[anywhere] + [in_vmem] * 3 + [anywhere] * 4,
        out_specs=[in_vmem] * 2,
        scratch_shapes=scratch,
        compiler_params=pltpu.CompilerParams(
            collective_id=0, has_side_effects=True, vmem_limit_bytes=58 * 2**20
        ),
    )(kspace, coil_maps, sampling, variation_weights, *[jnp.asarray(t) for t in tables])
    return image[:, :, None, :], residual[:, :, None, :]


def solution(mesh, gx=4, gz=8):
    gy = mesh.shape["coil"]

    def whole(kspace, coil_maps, sampling, variation_weights):
        length = kspace.shape[4]
        planes = length // (gx * gz * 2)
        sizes = (gx, gy, gz, planes, length, math.gcd(128, length, gx * gz * PAD))
        return jax.shard_map(
            partial(body, sizes),
            mesh=mesh,
            in_specs=(
                P(None, "coil", "slab", None, None),
                P(None, "coil", "slab", None, None),
                P("slab", None),
                P(None, "slab", "coil", None),
            ),
            out_specs=(P(None, "slab", "coil", None), P(None, "slab", "coil", None)),
            check_vma=False,
        )(kspace, coil_maps, sampling, variation_weights)

    return whole
```
